256 devices in a mesh: pair: 64 (over z, y, core), aux: 4 (over x).
Axes of the slice: x: 4, y: 4, z: 8, core: 2. Of those that a mesh axis runs over, the one named last changes fastest.
Arguments:
- blocks: bfloat16 [4096, 512, 128], P('pair', 'aux'), may hold values from -1.5 to 1.5
- pno_coef: bfloat16 [1024, 512, 128], P('pair'), may hold values from -0.25 to 0.25
- source_dev: int32 [1024, 8], replicated, may hold values from 0 to 63, all different within a row; in each aligned block of 16 rows (0 to 15, 16 to 31, ...) at most 3 rows name the same one
- block_pos: int32 [1024, 8], replicated, may hold values from 0 to 63
- pno_energy: float32 [1024, 128], P('pair'), may hold values from 0.2 to 2
- occ_energy: float32 [1024], P('pair'), may hold values from 0.3 to 1.2
- pno_count: int32 [1024], P('pair'), may hold values from 32 to 128
- neighbour: int32 [1024, 4], P('pair'), may hold values from 0 to 1023, as said below
- coupling: float32 [1024, 4], P('pair'), may hold values from -1 to 1
- intersection: float32 [1024, 4, 128, 128], P('pair'), may hold values from -0.5 to 0.5
Outputs:
- amplitudes: float32 [1024, 128, 128], P('pair')
- pair_energy: float32 [1024], P('pair')
The draws below stay inside these ranges and needn't reach their ends.
Inputs may be any that keep to these rules, and one draw needn't show every extreme that they name: `source_dev`: the 8 entries of a row are distinct. Within the rows of one index of pair (aligned blocks of 16 rows) no value appears more than 3 times, and in every draw some value appears exactly 3 times in some such block. neighbour[p, n] differs from p by 1 to 16; both ends of that reach occur in every draw.
All inputs are finite; a program needn't handle non-finite values.
Results may differ from the reference program's by a relative error of at most 0.0041.
Values may be sent and summed in bfloat16 or wider, within the bound.
A program may use at most 64 MiB of HBM per device.

```python
import math
import jax
import jax.numpy as jnp
import numpy as np
from jax import lax

PAIR_DEV = 16
BLK_DEV = 64
TILE = 128
DOM = 4
NPNO = 128
NB = 4
ITERS = 3
NPAIR = 1024
NBLK = 4096
NAUX = 512
CAP = 3


def draw_neighbour(key, part):
    key = jax.random.fold_in(key, 7)
    first_key, second_key = jax.random.split(key)
    reach = jax.random.randint(first_key, (NPAIR, NB), 1, PAIR_DEV + 1)
    direction = jax.random.randint(second_key, (NPAIR, NB), 0, 2) * 2 - 1
    pair_rows = jnp.arange(NPAIR, dtype=jnp.int32)[:, None]
    column = jnp.arange(NB, dtype=jnp.int32)[None, :]
    leading = (pair_rows % PAIR_DEV == 0) & (column == 0)
    trailing = (pair_rows % PAIR_DEV == PAIR_DEV - 1) & (column == 1)
    reach = jnp.where(leading | trailing, PAIR_DEV, reach)
    direction = jnp.where(leading, -1, jnp.where(trailing, 1, direction))
    target = pair_rows + direction * reach
    target = jnp.where(target < 0, pair_rows + reach, target)
    target = jnp.where(target >= NPAIR, pair_rows - reach, target)
    return target.astype(jnp.int32)


def plant(values, rng, low, top_value):
    longest = values.shape.index(max(values.shape))
    spots = []
    for shift in (0, 1):
        where = [jax.random.randint(jax.random.fold_in(rng, axis), (), 0, length) for axis, length in enumerate(values.shape)]
        where[longest] = (where[longest] + shift) % values.shape[longest]
        spots.append(tuple(where))
    return values.at[spots[0]].set(low).at[spots[1]].set(top_value)


def block_levels(own_key, shape, shards, least, largest):
    def one(axis_at, shards_of):
        heights = jax.random.uniform(jax.random.fold_in(jax.random.fold_in(own_key, 6), axis_at), (shards_of,), jnp.float32, least / len(shards), largest / len(shards))
        return jnp.repeat(jnp.exp(heights), shape[axis_at] // shards_of).reshape((-1,) + (1,) * (len(shape) - axis_at - 1))

    loudness = one(*shards[0])
    for cut in shards[1:]:
        loudness = loudness * one(*cut)
    return loudness


def deal_out(rng, own, number, rows, count, top, bound, skew):
    sequence = jax.random.permutation(rng, count)
    packed, ordinary = portions_of(count, rows * top, bound, skew, True), portions_of(count, rows * top, bound, skew, False)
    places = jnp.arange(count)

    def named(lengths, rotation):
        used = int((lengths > 0).sum())
        fixed = max(1, used // 4)
        moved = fixed + (places - fixed + rotation * (used - fixed)) % max(1, count - fixed)
        return jnp.zeros((count,), jnp.int32).at[sequence[jnp.where(places < fixed, places, moved)]].set(jnp.asarray(lengths, jnp.int32))

    lengths = jnp.where(number % 4 == 0, named(packed, number // 4), named(ordinary, number - number // 4 - 1))
    mixed = jax.random.permutation(jax.random.fold_in(own, 3), count)
    giver, receiver = mixed[0:count // 2 * 2:2], mixed[1:count // 2 * 2:2]
    slack = jnp.minimum(lengths[giver] - 1, bound - lengths[receiver]) // 2
    slack = jnp.where((giver == sequence[0]) | (receiver == sequence[0]) | (lengths[receiver] == 0), 0, jnp.maximum(slack, 0))
    moved = jax.random.randint(jax.random.fold_in(own, 4), (count // 2,), 0, 1 << 20) % (slack + 1)
    lengths = lengths.at[giver].add(-moved).at[receiver].add(moved)
    labels = jnp.searchsorted(jnp.cumsum(lengths), jnp.arange(rows * top), side="right").astype(jnp.int32)
    table = labels.reshape(top, rows).T
    table = table[jax.random.permutation(jax.random.fold_in(own, 1), rows)]
    rotation = jax.random.randint(jax.random.fold_in(own, 2), (rows, 1), 0, top)
    return jnp.take_along_axis(table, (jnp.arange(top)[None, :] + rotation) % top, axis=1)


def portions_of(number_of, total, limit, lean, full):
    loads = [(1 << 20) // math.isqrt(grade ** lean) + 1 for grade in range(1, number_of + 1)]
    largest = limit if full else min(limit, max(-(-total // number_of), total * loads[0] // sum(loads)))
    least = 1 if total - largest >= number_of - 1 else 0
    holding, surplus = [largest] + [least] * (number_of - 1), total - largest - least * (number_of - 1)
    while surplus > 0:
        movable = [i for i in range(1, number_of) if holding[i] < largest] or [i for i in range(1, number_of) if holding[i] < limit]
        pool, left = sum([loads[i] for i in movable]), surplus
        for i in movable:
            addition = min(limit - holding[i], max(1, left * loads[i] // pool), surplus)
            holding[i] = holding[i] + addition
            surplus = surplus - addition
    return np.array(holding)


def bell_draw(own_key, extent, width, most, pieces=(), kind=jnp.bfloat16):
    entries = jax.random.normal(own_key, extent, jnp.float32) * width
    if len(pieces) > 0:
        entries = block_levels(own_key, extent, pieces, -0.22, 0.18) * entries
    return jnp.clip(entries, min=-most, max=most).astype(kind)


def setup_inputs(seed: int = 0) -> dict:
    splits = jax.random.split(jax.random.key(seed), 11)
    blocks = bell_draw(splits[0], (NBLK, NAUX, TILE), 0.25, 1.5, ((0, 64), (1, 4)))
    pno_coef = bell_draw(splits[1], (NPAIR, DOM * TILE, NPNO), (DOM * TILE) ** -0.5, 0.25, ((0, 64),))
    source_dev_keys = jax.random.split(jax.random.fold_in(splits[2], 1), NPAIR // PAIR_DEV)
    source_dev_turns = jax.random.permutation(jax.random.fold_in(splits[2], 3), NPAIR // PAIR_DEV)
    source_dev = jax.vmap(lambda own, number: deal_out(jax.random.fold_in(splits[2], 2), own, number, PAIR_DEV, NPAIR // PAIR_DEV, 2 * DOM, CAP, 1))(source_dev_keys, source_dev_turns).reshape((NPAIR, 2 * DOM))
    block_pos = plant(jax.random.randint(splits[3], (NPAIR, 2 * DOM), 0, BLK_DEV), jax.random.fold_in(splits[3], 1), 0, BLK_DEV - 1).astype(jnp.int32)
    pno_energy = jnp.clip(jnp.exp(math.log(2.0) - 2.3025851 * jax.random.uniform(splits[4], (NPAIR, NPNO), jnp.float32) ** block_levels(splits[4], (NPAIR, NPNO), ((0, 64),), -0.2, 0.2)), 0.2, 2.0)
    occ_energy = jnp.clip(jnp.exp(math.log(1.2) - 1.3862944 * jax.random.uniform(splits[5], (NPAIR,), jnp.float32) ** block_levels(splits[5], (NPAIR,), ((0, 64),), -0.2, 0.2)), 0.3, 1.2)
    pno_count = plant(jax.random.randint(splits[6], (NPAIR,), NPNO // 4, NPNO + 1), jax.random.fold_in(splits[6], 1), NPNO // 4, NPNO).astype(jnp.int32)
    neighbour = draw_neighbour(jax.random.fold_in(splits[10], 71), 0)
    coupling = jnp.clip(jax.random.uniform(splits[8], (NPAIR, NB), jnp.float32, -1.0, 1.0) * block_levels(splits[8], (NPAIR, NB), ((0, 64),), -0.4, 0.0), -1.0, 1.0)
    intersection = bell_draw(splits[9], (NPAIR, NB, NPNO, NPNO), NPNO ** -0.5, 0.5, ((0, 64),), jnp.float32)
    return {"blocks": blocks, "pno_coef": pno_coef, "source_dev": source_dev, "block_pos": block_pos, "pno_energy": pno_energy, "occ_energy": occ_energy, "pno_count": pno_count, "neighbour": neighbour, "coupling": coupling, "intersection": intersection}


HIGH = lax.Precision.HIGHEST


def reference(blocks, pno_coef, source_dev, block_pos, pno_energy, occ_energy, pno_count, neighbour, coupling, intersection):
    block_ids = (source_dev * BLK_DEV + block_pos).astype(jnp.int32)
    groups = NPAIR // PAIR_DEV

    def build(item):
        group_ids, group_coef = item
        gathered = blocks[group_ids].astype(jnp.float32).reshape(PAIR_DEV, 2, DOM, NAUX, TILE)
        coefs = group_coef.astype(jnp.float32).reshape(PAIR_DEV, DOM, TILE, NPNO)
        projected = jnp.einsum("qmtxp,qtpn->qmxn", gathered, coefs, precision=HIGH).astype(jnp.bfloat16)
        projected = lax.optimization_barrier(projected).astype(jnp.float32)
        return jnp.einsum("qxa,qxb->qab", projected[:, 0], projected[:, 1], precision=HIGH)

    exchange_ints = lax.map(build, (block_ids.reshape(groups, PAIR_DEV, 2 * DOM),
                                    pno_coef.reshape(groups, PAIR_DEV, DOM * TILE, NPNO)))
    exchange_ints = exchange_ints.reshape(NPAIR, NPNO, NPNO)
    positions = jnp.arange(NPNO, dtype=jnp.int32)
    live = (positions[None, :] < pno_count[:, None]).astype(jnp.float32)
    mask = live[:, :, None] * live[:, None, :]
    denom = pno_energy[:, :, None] + pno_energy[:, None, :] + occ_energy[:, None, None]
    integrals = mask * exchange_ints
    amplitudes = -integrals / denom
    for sweep in range(ITERS):
        def couple(item):
            near_ids, weights, intersections = item
            near = amplitudes[near_ids]
            first = jnp.einsum("gnab,gnbc->gnac", intersections, near, precision=HIGH)
            second = jnp.einsum("gnac,gndc->gnad", first, intersections, precision=HIGH)
            return jnp.einsum("gn,gnad->gad", weights, second, precision=HIGH)

        coupled = lax.map(couple, (neighbour.reshape(groups, PAIR_DEV, NB),
                                   coupling.reshape(groups, PAIR_DEV, NB),
                                   intersection.reshape(groups, PAIR_DEV, NB, NPNO, NPNO)))
        coupled = coupled.reshape(NPAIR, NPNO, NPNO)
        amplitudes = mask * (coupled - integrals) / denom
    pair_energy = jnp.sum(integrals * (2.0 * amplitudes - jnp.swapaxes(amplitudes, 1, 2)), axis=(1, 2))
    return amplitudes, pair_energy
```

```python
import functools

import jax
import jax.numpy as jnp
from jax import lax
from jax.experimental import pallas as pl
from jax.experimental.pallas import tpu as pltpu
from jax.sharding import PartitionSpec as P

ITERS = 3
MESH = pl.DeviceIdType.MESH

PLANES = 8
COLS = 8
OWNERS = PLANES * COLS
AUXES = 4
PAIRS = 16
REQ = 8
TOTAL = PAIRS * REQ
TILE = 128
CAP = 3
DIRECT = 2
EXTRA = 2

VMEM_LIMIT = 56 * 2**20


def distance(step):
    dz, dy, _ = step
    return min(dz, PLANES - dz) + min(dy, 4 - dy)


STEPS = sorted(
    [(dz, dy, dc) for dz in range(PLANES) for dy in range(4) for dc in range(2) if (dz, dy, dc) != (0, 0, 0)],
    key=lambda s: -distance(s),
)


def exchange_kernel(
    send_pos, relay_row, land_row, blocks, coef_hbm, out,
    coef, outgoing, landing, relay_out, relay_in, extra_out, coef_sem, sems,
):
    me, ax = lax.axis_index("pair"), lax.axis_index("aux")
    plane, col = me // COLS, me % COLS
    y, core = col // 2, col % 2

    barrier = pltpu.get_barrier_semaphore()

    def greet(k, carry):
        pl.semaphore_signal(barrier, inc=1, device_id=(lax.rem(me + k, OWNERS), ax), device_id_type=MESH)
        return carry

    lax.fori_loop(1, OWNERS, greet, 0)
    coef_copy = pltpu.make_async_copy(coef_hbm, coef, coef_sem)
    coef_copy.start()

    def fill(k, carry):
        dst = lax.rem(me + k, OWNERS)
        for s in range(DIRECT):
            outgoing[DIRECT * k + s] = blocks[send_pos[dst * CAP + s]]
        return carry

    lax.fori_loop(0, OWNERS, fill, 0)

    def fill_relay(i, carry):
        k, b = i // PLANES, i % PLANES
        dst = b * COLS + lax.rem(col + k, COLS)
        relay_out[i] = blocks[send_pos[dst * CAP + DIRECT]]
        return carry

    lax.fori_loop(0, OWNERS, fill_relay, 0)
    for s in range(DIRECT):
        landing[s] = outgoing[s]
    for b in range(PLANES):
        relay_in[b] = relay_out[b]
    pl.semaphore_wait(barrier, OWNERS - 1)

    def direct(dst):
        to, back = lax.rem(dst - me + OWNERS, OWNERS), lax.rem(me - dst + OWNERS, OWNERS)
        return pltpu.make_async_remote_copy(
            src_ref=outgoing.at[pl.ds(DIRECT * to, DIRECT)],
            dst_ref=landing.at[pl.ds(DIRECT * back, DIRECT)],
            send_sem=sems.at[0], recv_sem=sems.at[1],
            device_id=(dst, ax), device_id_type=MESH,
        )

    def to_relay(k):
        return pltpu.make_async_remote_copy(
            src_ref=relay_out.at[pl.ds(PLANES * k, PLANES)],
            dst_ref=relay_in.at[pl.ds(PLANES * (COLS - k), PLANES)],
            send_sem=sems.at[2], recv_sem=sems.at[3],
            device_id=(plane * COLS + lax.rem(col + k, COLS), ax), device_id_type=MESH,
        )

    def from_relay(k):
        return pltpu.make_async_remote_copy(
            src_ref=extra_out.at[pl.ds(EXTRA * k, EXTRA)],
            dst_ref=landing.at[pl.ds(DIRECT * OWNERS + EXTRA * (PLANES - k), EXTRA)],
            send_sem=sems.at[4], recv_sem=sems.at[5],
            device_id=(lax.rem(plane + k, PLANES) * COLS + col, ax), device_id_type=MESH,
        )

    for k in range(1, COLS):
        to_relay(k).start()
    for dz, dy, dc in STEPS:
        direct(
            lax.rem(plane + dz, PLANES) * COLS + lax.rem(y + dy, 4) * 2 + lax.rem(core + dc, 2)
        ).start()

    def whole(source, target, first, count, sem):
        return pltpu.make_async_remote_copy(
            src_ref=source.at[pl.ds(first, count)], dst_ref=target.at[pl.ds(first, count)],
            send_sem=sems.at[sem], recv_sem=sems.at[sem + 1],
            device_id=(lax.rem(me + 1, OWNERS), ax), device_id_type=MESH,
        )

    relayed = whole(relay_out, relay_in, PLANES, PLANES * (COLS - 1), 2)
    relayed.wait_recv()
    for k in (4, 3, 5, 2, 6, 1, 7, 0):
        b = lax.rem(plane + k, PLANES)
        for e in range(EXTRA):
            block = relay_in[relay_row[b * EXTRA + e]]
            if k == 0:
                landing[DIRECT * OWNERS + e] = block
            else:
                extra_out[EXTRA * k + e] = block
        if k != 0:
            from_relay(k).start()

    coef_copy.wait()
    relayed.wait_send()
    sent = whole(outgoing, landing, DIRECT, DIRECT * (OWNERS - 1), 0)
    sent.wait_send()
    sent.wait_recv()
    extras = pltpu.make_async_remote_copy(
        src_ref=extra_out.at[pl.ds(EXTRA, EXTRA * (PLANES - 1))],
        dst_ref=landing.at[pl.ds(DIRECT * OWNERS + EXTRA, EXTRA * (PLANES - 1))],
        send_sem=sems.at[4], recv_sem=sems.at[5],
        device_id=(lax.rem(me + 1, OWNERS), ax), device_id_type=MESH,
    )
    extras.wait_send()
    extras.wait_recv()

    def build(q, carry):
        halves = []
        for m in range(2):
            total = None
            for t in range(REQ // 2):
                term = jnp.dot(
                    landing[land_row[q * REQ + m * (REQ // 2) + t]],
                    coef[q, t * TILE : (t + 1) * TILE, :],
                    preferred_element_type=jnp.float32,
                )
                total = term if total is None else total + term
            halves.append(total.astype(jnp.bfloat16))
        out[q] = lax.dot_general(
            halves[0], halves[1], (((0,), (0,)), ((), ())), preferred_element_type=jnp.float32
        )
        return carry

    lax.fori_loop(0, PAIRS, build, 0)


def exchange(blocks, coef, send_pos, relay_row, land_row):
    smem, vmem = pl.BlockSpec(memory_space=pltpu.SMEM), pl.BlockSpec(memory_space=pltpu.VMEM)
    tiles = lambda n: pltpu.VMEM((n, TILE, TILE), jnp.bfloat16)
    return pl.pallas_call(
        exchange_kernel,
        out_shape=jax.ShapeDtypeStruct((PAIRS, TILE, TILE), jnp.float32),
        in_specs=[smem, smem, smem, vmem, pl.BlockSpec(memory_space=pl.ANY)],
        out_specs=vmem,
        scratch_shapes=[
            pltpu.VMEM(coef.shape, jnp.bfloat16),
            tiles(DIRECT * OWNERS),
            tiles(DIRECT * OWNERS + EXTRA * PLANES),
            tiles(OWNERS),
            tiles(OWNERS),
            tiles(EXTRA * PLANES),
            pltpu.SemaphoreType.DMA,
            pltpu.SemaphoreType.DMA((6,)),
        ],
        compiler_params=pltpu.CompilerParams(
            collective_id=0, has_side_effects=True, vmem_limit_bytes=VMEM_LIMIT
        ),
    )(send_pos, relay_row, land_row, blocks, coef)


def padded_exchange(blocks, coef, send_pos, own_source, own_rank):
    incoming = lax.all_to_all(
        blocks[send_pos], "pair", split_axis=0, concat_axis=0, tiled=True
    )
    arrived = incoming.reshape((OWNERS * CAP,) + blocks.shape[1:])[own_source * CAP + own_rank]
    arrived = arrived.reshape((PAIRS, 2, REQ // 2) + blocks.shape[1:])
    coefs = coef.reshape(PAIRS, REQ // 2, TILE, TILE)
    projected = jnp.einsum(
        "qmtxp,qtpn->qmxn", arrived, coefs, preferred_element_type=jnp.float32
    ).astype(jnp.bfloat16)
    return jnp.einsum(
        "qxa,qxb->qab", projected[:, 0], projected[:, 1], preferred_element_type=jnp.float32
    )


def route(source_dev, block_pos, me):
    plane, col = me // COLS, me % COLS
    source = source_dev.reshape(OWNERS, TOTAL)
    position = block_pos.reshape(OWNERS, TOTAL)
    slots = jnp.arange(CAP, dtype=jnp.int32)
    devices = jnp.arange(OWNERS, dtype=jnp.int32)
    wanted = source == me
    ranking = jnp.cumsum(wanted.astype(jnp.int32), axis=1) - 1
    chosen = wanted[:, None, :] & (ranking[:, None, :] == slots[None, :, None])
    send_pos = jnp.sum(jnp.where(chosen, position[:, None, :], 0), axis=2)
    taken = jnp.sum((source[:, None, :] == devices[None, :, None]).astype(jnp.int32), axis=2)
    third = (taken > DIRECT).astype(jnp.int32)
    fits = jnp.max(jnp.sum(third.reshape(OWNERS, PLANES, COLS), axis=2)) <= EXTRA
    own_source = lax.dynamic_index_in_dim(source, me, 0, keepdims=False)
    order = jnp.arange(TOTAL, dtype=jnp.int32)
    earlier = (own_source[None, :] == own_source[:, None]) & (order[None, :] < order[:, None])
    own_rank = jnp.sum(earlier.astype(jnp.int32), axis=1)
    own_third = lax.dynamic_index_in_dim(third, me, 0, keepdims=False)
    before = (devices[None, :] < own_source[:, None]) & (
        devices[None, :] // COLS == own_source[:, None] // COLS
    )
    extra_rank = jnp.sum(jnp.where(before, own_third[None, :], 0), axis=1)
    extra_row = (
        DIRECT * OWNERS
        + lax.rem(own_source // COLS - plane + PLANES, PLANES) * EXTRA
        + jnp.minimum(extra_rank, EXTRA - 1)
    )
    direct_row = lax.rem(own_source - me + OWNERS, OWNERS) * DIRECT + own_rank
    land_row = jnp.where(own_rank >= DIRECT, extra_row, direct_row)
    column = lax.dynamic_index_in_dim(third.reshape(PLANES, COLS, PLANES, COLS), col, 1, keepdims=False)
    column = lax.dynamic_index_in_dim(column, plane, 1, keepdims=False)
    cols = jnp.arange(COLS, dtype=jnp.int32)
    place = jnp.cumsum(column, axis=1) - column
    hit = (column == 1)[:, None, :] & (place[:, None, :] == jnp.arange(EXTRA)[None, :, None])
    back = lax.rem(cols - col + COLS, COLS)
    relay_row = jnp.sum(jnp.where(hit, back[None, None, :], 0), axis=2) * PLANES + cols[:, None]
    return send_pos, relay_row, land_row, own_source, own_rank, fits


def sweep_kernel(
    near, weight, count, occ, partial, energy, inter_hbm, amp, pair_energy,
    inter, vecs, window0, window1, window2, integ, inverse, sums, inter_sem, rs_send, rs_recv, ag_send, ag_recv, halo_send, halo_recv,
):
    me, ax = lax.axis_index("pair"), lax.axis_index("aux")
    left, right = lax.rem(me + OWNERS - 1, OWNERS), lax.rem(me + 1, OWNERS)
    chunk = PAIRS // AUXES
    own = pl.multiple_of(ax * chunk, chunk)
    peers = [lax.rem(ax + r, AUXES) for r in range(AUXES)]
    windows = (window0, window1, window2)

    barrier = pltpu.get_barrier_semaphore()
    for r in range(1, AUXES):
        pl.semaphore_signal(barrier, inc=1, device_id=(me, peers[r]), device_id_type=MESH)
    for side in (left, right):
        pl.semaphore_signal(barrier, inc=1, device_id=(side, ax), device_id_type=MESH)
    inter_copy = pltpu.make_async_copy(inter_hbm, inter, inter_sem)
    inter_copy.start()
    pl.semaphore_wait(barrier, AUXES + 1)

    def reduce_copy(r):
        return pltpu.make_async_remote_copy(
            src_ref=partial.at[pl.ds(peers[r] * chunk, chunk)], dst_ref=sums.at[AUXES - 1 - r],
            send_sem=rs_send.at[r - 1], recv_sem=rs_recv.at[AUXES - 1 - r],
            device_id=(me, peers[r]), device_id_type=MESH,
        )

    def gather_copy(r):
        return pltpu.make_async_remote_copy(
            src_ref=integ.at[pl.ds(own, chunk)], dst_ref=integ.at[pl.ds(own, chunk)],
            send_sem=ag_send.at[r - 1], recv_sem=ag_recv.at[AUXES - 1 - r],
            device_id=(me, peers[r]), device_id_type=MESH,
        )

    def halo_copy(sweep, first, size, side):
        target = first + 2 * PAIRS if side == 0 else first
        return pltpu.make_async_remote_copy(
            src_ref=windows[sweep].at[pl.ds(PAIRS + first, size)],
            dst_ref=windows[sweep].at[pl.ds(target, size)],
            send_sem=halo_send.at[sweep, side], recv_sem=halo_recv.at[sweep, side],
            device_id=(left if side == 0 else right, ax), device_id_type=MESH,
        )

    def halo_wait(sweep):
        for side in range(2):
            done = pltpu.make_async_remote_copy(
                src_ref=windows[sweep].at[pl.ds(PAIRS, PAIRS)],
                dst_ref=windows[sweep].at[pl.ds(2 * PAIRS if side == 0 else 0, PAIRS)],
                send_sem=halo_send.at[sweep, side], recv_sem=halo_recv.at[sweep, side],
                device_id=(left if side == 0 else right, ax), device_id_type=MESH,
            )
            done.wait_send()
            done.wait_recv()

    for r in (2, 1, 3):
        reduce_copy(r).start()

    rows = lax.broadcasted_iota(jnp.int32, (TILE, TILE), 0)
    columns = lax.broadcasted_iota(jnp.int32, (TILE, TILE), 1)

    def denominators(q, carry):
        e = energy[pl.ds(q, 1), :]
        across = jnp.broadcast_to(e, (TILE, TILE))
        denom = across + across.T + occ[q]
        live = (rows < count[q]) & (columns < count[q])
        inverse[q] = jnp.where(live, 1.0 / denom, 0.0)
        return carry

    lax.fori_loop(0, PAIRS, denominators, 0)
    inter_copy.wait()

    def narrow(q, carry):
        vecs[q] = inter[q].astype(jnp.bfloat16)
        return carry

    lax.fori_loop(0, PAIRS, narrow, 0)

    for r in (1, 3, 2):
        reduce_copy(r).wait_recv()

    def add(i, carry):
        q = own + i
        live = (rows < count[q]) & (columns < count[q])
        integ[q] = jnp.where(live, partial[q] + sums[0, i] + sums[1, i] + sums[2, i], 0.0)
        return carry

    lax.fori_loop(0, chunk, add, 0)
    for r in (2, 1, 3):
        gather_copy(r).start()

    def first_amplitudes(start):
        def body(i, carry):
            q = start + i
            window0[PAIRS + q] = (-integ[q] * inverse[q]).astype(jnp.bfloat16)
            return carry

        lax.fori_loop(0, chunk, body, 0)
        for side in range(2):
            halo_copy(0, start, chunk, side).start()

    first_amplitudes(own)
    for r in (1, 3, 2):
        arrived = pltpu.make_async_remote_copy(
            src_ref=integ.at[pl.ds(own, chunk)], dst_ref=integ.at[pl.ds(peers[r] * chunk, chunk)],
            send_sem=ag_send.at[r - 1], recv_sem=ag_recv.at[r - 1],
            device_id=(me, peers[r]), device_id_type=MESH,
        )
        arrived.wait_recv()
        first_amplitudes(pl.multiple_of(peers[r] * chunk, chunk))

    for sweep in range(ITERS):
        halo_wait(sweep)

        def update(q, sweep=sweep):
            total = None
            for n in range(4):
                v = vecs[q, n]
                first = jnp.dot(v, windows[sweep][near[q * 4 + n]], preferred_element_type=jnp.float32)
                first = (first * weight[q * 4 + n]).astype(jnp.bfloat16)
                second = lax.dot_general(
                    first, v, (((1,), (1,)), ((), ())), preferred_element_type=jnp.float32
                )
                total = second if total is None else total + second
            integrals = integ[q]
            current = (total - integrals) * inverse[q]
            if sweep < ITERS - 1:
                windows[sweep + 1][PAIRS + q] = current.astype(jnp.bfloat16)
            else:
                amp[q] = current
                pair_energy[q] = jnp.sum(integrals * (2.0 * current - current.T))

        for j in range(AUXES):
            def body(i, carry, j=j):
                update(j * chunk + i)
                return carry

            lax.fori_loop(0, chunk, body, 0)
            if sweep < ITERS - 1:
                for side in range(2):
                    halo_copy(sweep + 1, j * chunk, chunk, side).start()

    for r in range(1, AUXES):
        reduce_copy(r).wait_send()
        gather_copy(r).wait_send()


def sweeps(partial, energy, occ, count, near, weight, inter):
    smem, vmem = pl.BlockSpec(memory_space=pltpu.SMEM), pl.BlockSpec(memory_space=pltpu.VMEM)
    f32, bf16 = jnp.float32, jnp.bfloat16
    chunk = PAIRS // AUXES
    dma = pltpu.SemaphoreType.DMA
    return pl.pallas_call(
        sweep_kernel,
        out_shape=(
            jax.ShapeDtypeStruct((PAIRS, TILE, TILE), f32),
            jax.ShapeDtypeStruct((PAIRS,), f32),
        ),
        in_specs=[smem, smem, smem, smem, vmem, vmem, pl.BlockSpec(memory_space=pl.ANY)],
        out_specs=(vmem, smem),
        scratch_shapes=[
            pltpu.VMEM(inter.shape, f32),
            pltpu.VMEM(inter.shape, bf16),
            *[pltpu.VMEM((3 * PAIRS, TILE, TILE), bf16)] * ITERS,
            pltpu.VMEM((PAIRS, TILE, TILE), f32),
            pltpu.VMEM((PAIRS, TILE, TILE), f32),
            pltpu.VMEM((AUXES - 1, chunk, TILE, TILE), f32),
            dma,
            dma((AUXES - 1,)), dma((AUXES - 1,)), dma((AUXES - 1,)), dma((AUXES - 1,)),
            dma((ITERS, 2)), dma((ITERS, 2)),
        ],
        compiler_params=pltpu.CompilerParams(
            collective_id=1, has_side_effects=True, vmem_limit_bytes=VMEM_LIMIT
        ),
    )(near, weight, count, occ, partial, energy, inter)


def shards(
    blocks, pno_coef, source_dev, block_pos, pno_energy, occ_energy, pno_count, neighbour, coupling, intersection,
):
    me = lax.axis_index("pair")
    send_pos, relay_row, land_row, own_source, own_rank, fits = route(source_dev, block_pos, me)
    partial = lax.cond(
        fits,
        lambda: exchange(blocks, pno_coef, send_pos.reshape(-1), relay_row.reshape(-1), land_row),
        lambda: padded_exchange(blocks, pno_coef, send_pos, own_source, own_rank),
    )
    near = neighbour - (me - 1) * PAIRS
    return sweeps(
        partial, pno_energy, occ_energy, pno_count, near.reshape(-1), coupling.reshape(-1), intersection
    )


def solution(mesh):
    return jax.shard_map(
        shards,
        mesh=mesh,
        in_specs=(
            P("pair", "aux", None),
            P("pair", None, None),
            P(),
            P(),
            P("pair", None),
            P("pair"),
            P("pair"),
            P("pair", None),
            P("pair", None),
            P("pair", None, None, None),
        ),
        out_specs=(P("pair", None, None), P("pair")),
        check_vma=False,
    )
```

```python
import functools
import types

import jax
import jax.numpy as jnp
from jax import lax
from jax.experimental import pallas as pl
from jax.experimental.pallas import tpu as pltpu
from jax.sharding import PartitionSpec as P

ITERS = 3
MESH = pl.DeviceIdType.MESH

PLANES = 8
COLS = 8
OWNERS = PLANES * COLS
AUXES = 4
PAIRS = 16
REQ = 8
DOM = 4
BLOCKS = 64
TOTAL = PAIRS * REQ
TILE = 128
CAP = 3
DIRECT = 2
EXTRA = 2

VMEM_LIMIT = 56 * 2**20
CHUNK = PAIRS // AUXES


def distance(step):
    dz, dy, _ = step
    return min(dz, PLANES - dz) + min(dy, 4 - dy)


STEPS = sorted(
    [(dz, dy, dc) for dz in range(PLANES) for dy in range(4) for dc in range(2) if (dz, dy, dc) != (0, 0, 0)],
    key=lambda s: -distance(s),
)


SCRATCH = {
    "inter": ((PAIRS, 4, TILE, TILE), jnp.float32),
    "vecs": ((PAIRS, TILE, 4 * TILE), jnp.bfloat16),
    "weighted": ((PAIRS, TILE, 4 * TILE), jnp.bfloat16),
    "window0": ((3 * PAIRS, TILE, TILE), jnp.bfloat16),
    "window1": ((3 * PAIRS, TILE, TILE), jnp.bfloat16),
    "window2": ((3 * PAIRS, TILE, TILE), jnp.bfloat16),
    "integ": ((PAIRS, TILE, TILE), jnp.float32),
    "inverse": ((PAIRS, TILE, TILE), jnp.float32),
    "own_part": ((CHUNK, TILE, TILE), jnp.float32),
    "high_out": ((AUXES - 1, CHUNK, TILE, TILE), jnp.bfloat16),
    "low_out": ((AUXES - 1, CHUNK, TILE, TILE), jnp.bfloat16),
    "high_in": ((AUXES - 1, CHUNK, TILE, TILE), jnp.bfloat16),
    "low_in": ((AUXES - 1, CHUNK, TILE, TILE), jnp.bfloat16),
    "high": ((PAIRS, TILE, TILE), jnp.bfloat16),
    "low": ((PAIRS, TILE, TILE), jnp.bfloat16),
    "local_sem": (2,),
    "x_send": (4, AUXES - 1),
    "x_recv": (4, AUXES - 1),
    "halo_send": (ITERS, 2),
    "halo_recv": (ITERS, 2),
}
EXCHANGE_SCRATCH = {
    "coef": ((PAIRS, DOM * TILE, TILE), jnp.bfloat16),
    "outgoing": ((DIRECT * OWNERS, TILE, TILE), jnp.bfloat16),
    "landing": ((DIRECT * OWNERS + EXTRA * PLANES, TILE, TILE), jnp.bfloat16),
    "relay_out": ((OWNERS, TILE, TILE), jnp.bfloat16),
    "relay_in": ((OWNERS, TILE, TILE), jnp.bfloat16),
    "extra_out": ((EXTRA * PLANES, TILE, TILE), jnp.bfloat16),
    "block_sem": (6,),
}
SEND, RELAY, LAND = 0, OWNERS * CAP, OWNERS * CAP + PLANES * EXTRA
NEAR = LAND + TOTAL
HIGH_SUM, HIGH_ALL, LOW_SUM, LOW_ALL = range(4)


def kernel(exchanging, *refs):
    names = ["table", "count", "occ", "source", "coef_hbm", "energy", "coupling", "inter_hbm", "amp", "pair_energy"]
    names += list(SCRATCH) + (list(EXCHANGE_SCRATCH) if exchanging else [])
    if not exchanging:
        names.remove("coef_hbm")
    r = types.SimpleNamespace(**dict(zip(names, refs, strict=True)))
    me, ax = lax.axis_index("pair"), lax.axis_index("aux")
    plane, col = me // COLS, me % COLS
    y, core = col // 2, col % 2
    left, right = lax.rem(me + OWNERS - 1, OWNERS), lax.rem(me + 1, OWNERS)
    own = pl.multiple_of(ax * CHUNK, CHUNK)
    peers = [lax.rem(ax + k, AUXES) for k in range(AUXES)]
    windows = (r.window0, r.window1, r.window2)

    barrier = pltpu.get_barrier_semaphore()
    for k in range(1, AUXES):
        pl.semaphore_signal(barrier, inc=1, device_id=(me, peers[k]), device_id_type=MESH)
    if exchanging:

        def greet(k, carry):
            pl.semaphore_signal(barrier, inc=1, device_id=(lax.rem(me + k, OWNERS), ax), device_id_type=MESH)
            return carry

        lax.fori_loop(1, OWNERS, greet, 0)
        greeted = AUXES - 1 + OWNERS - 1
    else:
        for side in (left, right):
            pl.semaphore_signal(barrier, inc=1, device_id=(side, ax), device_id_type=MESH)
        greeted = AUXES - 1 + 2

    inter_copy = pltpu.make_async_copy(r.inter_hbm, r.inter, r.local_sem.at[0])
    if exchanging:
        coef_copy = pltpu.make_async_copy(r.coef_hbm, r.coef, r.local_sem.at[1])

    rows = lax.broadcasted_iota(jnp.int32, (TILE, TILE), 0)
    columns = lax.broadcasted_iota(jnp.int32, (TILE, TILE), 1)

    def masked(q, values):
        return jnp.where((rows < r.count[q]) & (columns < r.count[q]), values, 0.0)

    def prepare():
        def denominators(q, carry):
            across = jnp.broadcast_to(r.energy[pl.ds(q, 1), :], (TILE, TILE))
            r.inverse[q] = masked(q, 1.0 / (across + across.T + r.occ[q]))
            return carry

        lax.fori_loop(0, PAIRS, denominators, 0)
        inter_copy.wait()

        def narrow(q, carry):
            for n in range(4):
                v = r.inter[q, n]
                cut = slice(n * TILE, (n + 1) * TILE)
                r.vecs[q, :, cut] = v.astype(jnp.bfloat16)
                r.weighted[q, :, cut] = (v * r.coupling[pl.ds(q, 1), n : n + 1]).astype(jnp.bfloat16)
            return carry

        lax.fori_loop(0, PAIRS, narrow, 0)

    if exchanging:
        blocks, outgoing, landing = r.source, r.outgoing, r.landing

        def fill(k, carry):
            dst = lax.rem(me + k, OWNERS)
            for s in range(DIRECT):
                outgoing[DIRECT * k + s] = blocks[r.table[SEND + dst * CAP + s]]
            return carry

        def fill_relay(i, carry):
            k, b = i // PLANES, i % PLANES
            dst = b * COLS + lax.rem(col + k, COLS)
            r.relay_out[i] = blocks[r.table[SEND + dst * CAP + DIRECT]]
            return carry

        lax.fori_loop(0, OWNERS, fill, 0)
        lax.fori_loop(0, OWNERS, fill_relay, 0)
        for s in range(DIRECT):
            landing[s] = outgoing[s]
        for b in range(PLANES):
            r.relay_in[b] = r.relay_out[b]

        def whole(source, target, first, count, sem):
            return pltpu.make_async_remote_copy(
                src_ref=source.at[pl.ds(first, count)], dst_ref=target.at[pl.ds(first, count)],
                send_sem=r.block_sem.at[sem], recv_sem=r.block_sem.at[sem + 1],
                device_id=(right, ax), device_id_type=MESH,
            )

        def direct(dst):
            to, back = lax.rem(dst - me + OWNERS, OWNERS), lax.rem(me - dst + OWNERS, OWNERS)
            return pltpu.make_async_remote_copy(
                src_ref=outgoing.at[pl.ds(DIRECT * to, DIRECT)],
                dst_ref=landing.at[pl.ds(DIRECT * back, DIRECT)],
                send_sem=r.block_sem.at[0], recv_sem=r.block_sem.at[1],
                device_id=(dst, ax), device_id_type=MESH,
            )

        def to_relay(k):
            return pltpu.make_async_remote_copy(
                src_ref=r.relay_out.at[pl.ds(PLANES * k, PLANES)],
                dst_ref=r.relay_in.at[pl.ds(PLANES * (COLS - k), PLANES)],
                send_sem=r.block_sem.at[2], recv_sem=r.block_sem.at[3],
                device_id=(plane * COLS + lax.rem(col + k, COLS), ax), device_id_type=MESH,
            )

        def from_relay(k):
            return pltpu.make_async_remote_copy(
                src_ref=r.extra_out.at[pl.ds(EXTRA * k, EXTRA)],
                dst_ref=landing.at[pl.ds(DIRECT * OWNERS + EXTRA * (PLANES - k), EXTRA)],
                send_sem=r.block_sem.at[4], recv_sem=r.block_sem.at[5],
                device_id=(lax.rem(plane + k, PLANES) * COLS + col, ax), device_id_type=MESH,
            )

        pl.semaphore_wait(barrier, greeted)
        for k in range(1, COLS):
            to_relay(k).start()
        for dz, dy, dc in STEPS:
            direct(
                lax.rem(plane + dz, PLANES) * COLS + lax.rem(y + dy, 4) * 2 + lax.rem(core + dc, 2)
            ).start()
        inter_copy.start()
        coef_copy.start()
        prepare()

        relayed = whole(r.relay_out, r.relay_in, PLANES, PLANES * (COLS - 1), 2)
        relayed.wait_recv()
        for k in (4, 3, 5, 2, 6, 1, 7, 0):
            b = lax.rem(plane + k, PLANES)
            for e in range(EXTRA):
                block = r.relay_in[r.table[RELAY + b * EXTRA + e]]
                if k == 0:
                    landing[DIRECT * OWNERS + e] = block
                else:
                    r.extra_out[EXTRA * k + e] = block
            if k != 0:
                from_relay(k).start()

        coef_copy.wait()
        relayed.wait_send()
        sent = whole(outgoing, landing, DIRECT, DIRECT * (OWNERS - 1), 0)
        sent.wait_send()
        sent.wait_recv()
        extras = pltpu.make_async_remote_copy(
            src_ref=r.extra_out.at[pl.ds(EXTRA, EXTRA * (PLANES - 1))],
            dst_ref=landing.at[pl.ds(DIRECT * OWNERS + EXTRA, EXTRA * (PLANES - 1))],
            send_sem=r.block_sem.at[4], recv_sem=r.block_sem.at[5],
            device_id=(right, ax), device_id_type=MESH,
        )
        extras.wait_send()
        extras.wait_recv()

        def part(q):
            rows_of = [
                jnp.concatenate(
                    [landing[r.table[LAND + q * REQ + m * DOM + t]] for t in range(DOM)], axis=1
                )
                for m in range(2)
            ]
            projected = jnp.dot(
                jnp.concatenate(rows_of, axis=0), r.coef[q], preferred_element_type=jnp.float32
            ).astype(jnp.bfloat16)
            return lax.dot_general(
                projected[:TILE], projected[TILE:], (((0,), (0,)), ((), ())),
                preferred_element_type=jnp.float32,
            )

    else:
        inter_copy.start()
        prepare()
        pl.semaphore_wait(barrier, greeted)

        def part(q):
            return r.source[q]

    def summed(kind, k):
        out, into = (r.high_out, r.high_in) if kind == HIGH_SUM else (r.low_out, r.low_in)
        return pltpu.make_async_remote_copy(
            src_ref=out.at[k - 1], dst_ref=into.at[AUXES - 1 - k],
            send_sem=r.x_send.at[kind, k - 1], recv_sem=r.x_recv.at[kind, AUXES - 1 - k],
            device_id=(me, peers[k]), device_id_type=MESH,
        )

    def spread(kind, k):
        values = r.high if kind == HIGH_ALL else r.low
        return pltpu.make_async_remote_copy(
            src_ref=values.at[pl.ds(own, CHUNK)], dst_ref=values.at[pl.ds(own, CHUNK)],
            send_sem=r.x_send.at[kind, k - 1], recv_sem=r.x_recv.at[kind, AUXES - 1 - k],
            device_id=(me, peers[k]), device_id_type=MESH,
        )

    def wait_summed(kind):
        into = r.high_in if kind == HIGH_SUM else r.low_in
        for k in range(1, AUXES):
            pltpu.make_async_remote_copy(
                src_ref=into.at[k - 1], dst_ref=into.at[k - 1],
                send_sem=r.x_send.at[kind, k - 1], recv_sem=r.x_recv.at[kind, k - 1],
                device_id=(me, peers[k]), device_id_type=MESH,
            ).wait_recv()

    def wait_spread(kind, k):
        values = r.high if kind == HIGH_ALL else r.low
        theirs = values.at[pl.ds(peers[k] * CHUNK, CHUNK)]
        pltpu.make_async_remote_copy(
            src_ref=theirs, dst_ref=theirs,
            send_sem=r.x_send.at[kind, k - 1], recv_sem=r.x_recv.at[kind, k - 1],
            device_id=(me, peers[k]), device_id_type=MESH,
        ).wait_recv()

    def halo(sweep, first, size, side):
        target = first + 2 * PAIRS if side == 0 else first
        return pltpu.make_async_remote_copy(
            src_ref=windows[sweep].at[pl.ds(PAIRS + first, size)],
            dst_ref=windows[sweep].at[pl.ds(target, size)],
            send_sem=r.halo_send.at[sweep, side], recv_sem=r.halo_recv.at[sweep, side],
            device_id=(left if side == 0 else right, ax), device_id_type=MESH,
        )

    def wait_halo(sweep):
        for side in range(2):
            done = pltpu.make_async_remote_copy(
                src_ref=windows[sweep].at[pl.ds(PAIRS, PAIRS)],
                dst_ref=windows[sweep].at[pl.ds(2 * PAIRS if side == 0 else 0, PAIRS)],
                send_sem=r.halo_send.at[sweep, side], recv_sem=r.halo_recv.at[sweep, side],
                device_id=(left if side == 0 else right, ax), device_id_type=MESH,
            )
            done.wait_send()
            done.wait_recv()

    for k in (2, 1, 3):

        def give(h, carry, k=k):
            for i in (2 * h, 2 * h + 1):
                values = part(peers[k] * CHUNK + i)
                top = values.astype(jnp.bfloat16)
                r.high_out[k - 1, i] = top
                r.low_out[k - 1, i] = (values - top.astype(jnp.float32)).astype(jnp.bfloat16)
            return carry

        lax.fori_loop(0, CHUNK // 2, give, 0)
        summed(HIGH_SUM, k).start()

    def keep(h, carry):
        for i in (2 * h, 2 * h + 1):
            r.own_part[i] = part(own + i)
        return carry

    lax.fori_loop(0, CHUNK // 2, keep, 0)
    wait_summed(HIGH_SUM)

    def add_high(i, carry):
        values = r.own_part[i]
        for k in range(AUXES - 1):
            values = values + r.high_in[k, i].astype(jnp.float32)
        r.high[own + i] = masked(own + i, values).astype(jnp.bfloat16)
        return carry

    lax.fori_loop(0, CHUNK, add_high, 0)
    for k in (2, 1, 3):
        spread(HIGH_ALL, k).start()

    def first_amplitudes(start):
        def body(i, carry):
            q = start + i
            windows[0][PAIRS + q] = (-r.high[q].astype(jnp.float32) * r.inverse[q]).astype(jnp.bfloat16)
            return carry

        lax.fori_loop(0, CHUNK, body, 0)
        for side in range(2):
            halo(0, start, CHUNK, side).start()

    first_amplitudes(own)
    for k in (2, 1, 3):
        summed(LOW_SUM, k).start()
    for k in (1, 3, 2):
        wait_spread(HIGH_ALL, k)
        first_amplitudes(pl.multiple_of(peers[k] * CHUNK, CHUNK))
    wait_summed(LOW_SUM)

    def add_low(i, carry):
        values = r.own_part[i]
        for k in range(AUXES - 1):
            values = values + r.high_in[k, i].astype(jnp.float32)
        for k in range(AUXES - 1):
            values = values + r.low_in[k, i].astype(jnp.float32)
        top = r.high[own + i].astype(jnp.float32)
        r.low[own + i] = (masked(own + i, values) - top).astype(jnp.bfloat16)
        return carry

    lax.fori_loop(0, CHUNK, add_low, 0)
    for k in (2, 1, 3):
        spread(LOW_ALL, k).start()

    for sweep in range(ITERS):
        wait_halo(sweep)
        if sweep == 0:
            for k in (1, 3, 2):
                wait_spread(LOW_ALL, k)

        def update(q, sweep=sweep):
            firsts = [
                jnp.dot(
                    r.weighted[q, :, n * TILE : (n + 1) * TILE],
                    windows[sweep][r.table[NEAR + q * 4 + n]],
                    preferred_element_type=jnp.float32,
                ).astype(jnp.bfloat16)
                for n in range(4)
            ]
            coupled = lax.dot_general(
                jnp.concatenate(firsts, axis=1), r.vecs[q], (((1,), (1,)), ((), ())),
                preferred_element_type=jnp.float32,
            )
            if sweep == 0:
                integrals = r.high[q].astype(jnp.float32) + r.low[q].astype(jnp.float32)
                r.integ[q] = integrals
            else:
                integrals = r.integ[q]
            current = (coupled - integrals) * r.inverse[q]
            if sweep < ITERS - 1:
                windows[sweep + 1][PAIRS + q] = current.astype(jnp.bfloat16)
            else:
                r.amp[q] = current
                r.pair_energy[q] = jnp.sum(integrals * (2.0 * current - current.T))

        def some(j, carry, sweep=sweep):
            for i in range(CHUNK):
                update(j * CHUNK + i)
            if sweep < ITERS - 1:
                for side in range(2):
                    halo(sweep + 1, pl.multiple_of(j * CHUNK, CHUNK), CHUNK, side).start()
            return carry

        lax.fori_loop(0, PAIRS // CHUNK, some, 0)

    for k in range(1, AUXES):
        for kind in (HIGH_SUM, LOW_SUM):
            summed(kind, k).wait_send()
        for kind in (HIGH_ALL, LOW_ALL):
            spread(kind, k).wait_send()


def run_kernel(exchanging, table, count, occ, source, coef, energy, coupling, inter):
    smem, vmem = pl.BlockSpec(memory_space=pltpu.SMEM), pl.BlockSpec(memory_space=pltpu.VMEM)
    hbm = pl.BlockSpec(memory_space=pl.ANY)
    scratch = dict(SCRATCH, **(EXCHANGE_SCRATCH if exchanging else {}))
    return pl.pallas_call(
        functools.partial(kernel, exchanging),
        out_shape=(
            jax.ShapeDtypeStruct((PAIRS, TILE, TILE), jnp.float32),
            jax.ShapeDtypeStruct((PAIRS,), jnp.float32),
        ),
        in_specs=[smem, smem, smem, vmem] + [hbm] * exchanging + [vmem, vmem, hbm],
        out_specs=(vmem, smem),
        scratch_shapes=[
            pltpu.SemaphoreType.DMA(v) if isinstance(v[0], int) else pltpu.VMEM(*v) for v in scratch.values()
        ],
        compiler_params=pltpu.CompilerParams(
            collective_id=0 if exchanging else 1, has_side_effects=True, vmem_limit_bytes=VMEM_LIMIT
        ),
    )(*([table, count, occ, source] + [coef] * exchanging + [energy, coupling, inter]))


def padded_exchange(blocks, coef, send_pos, own_source, own_rank):
    incoming = lax.all_to_all(
        blocks[send_pos], "pair", split_axis=0, concat_axis=0, tiled=True
    )
    arrived = incoming.reshape((OWNERS * CAP,) + blocks.shape[1:])[own_source * CAP + own_rank]
    arrived = arrived.reshape((PAIRS, 2, DOM) + blocks.shape[1:])
    coefs = coef.reshape(PAIRS, DOM, TILE, TILE)
    projected = jnp.einsum(
        "qmtxp,qtpn->qmxn", arrived, coefs, preferred_element_type=jnp.float32
    ).astype(jnp.bfloat16)
    return jnp.einsum(
        "qxa,qxb->qab", projected[:, 0], projected[:, 1], preferred_element_type=jnp.float32
    )


def route(source_dev, block_pos, me):
    plane, col = me // COLS, me % COLS
    both = (source_dev * BLOCKS + block_pos).reshape(OWNERS, TOTAL)
    source, position = both // BLOCKS, both % BLOCKS
    slots = jnp.arange(CAP, dtype=jnp.int32)
    devices = jnp.arange(OWNERS, dtype=jnp.int32)
    wanted = source == me
    ranking = jnp.cumsum(wanted.astype(jnp.int32), axis=1) - 1
    chosen = wanted[:, None, :] & (ranking[:, None, :] == slots[None, :, None])
    send_pos = jnp.sum(jnp.where(chosen, position[:, None, :], 0), axis=2)
    taken = jnp.sum((source[:, None, :] == devices[None, :, None]).astype(jnp.int32), axis=2)
    third = (taken > DIRECT).astype(jnp.int32)
    fits = jnp.max(jnp.sum(third.reshape(OWNERS, PLANES, COLS), axis=2)) <= EXTRA
    own_source = lax.dynamic_index_in_dim(source, me, 0, keepdims=False)
    order = jnp.arange(TOTAL, dtype=jnp.int32)
    earlier = (own_source[None, :] == own_source[:, None]) & (order[None, :] < order[:, None])
    own_rank = jnp.sum(earlier.astype(jnp.int32), axis=1)
    own_third = lax.dynamic_index_in_dim(third, me, 0, keepdims=False)
    before = (devices[None, :] < own_source[:, None]) & (
        devices[None, :] // COLS == own_source[:, None] // COLS
    )
    extra_rank = jnp.sum(jnp.where(before, own_third[None, :], 0), axis=1)
    extra_row = (
        DIRECT * OWNERS
        + lax.rem(own_source // COLS - plane + PLANES, PLANES) * EXTRA
        + jnp.minimum(extra_rank, EXTRA - 1)
    )
    direct_row = lax.rem(own_source - me + OWNERS, OWNERS) * DIRECT + own_rank
    land_row = jnp.where(own_rank >= DIRECT, extra_row, direct_row)
    column = lax.dynamic_index_in_dim(third.reshape(PLANES, COLS, PLANES, COLS), col, 1, keepdims=False)
    column = lax.dynamic_index_in_dim(column, plane, 1, keepdims=False)
    cols = jnp.arange(COLS, dtype=jnp.int32)
    place = jnp.cumsum(column, axis=1) - column
    hit = (column == 1)[:, None, :] & (place[:, None, :] == jnp.arange(EXTRA)[None, :, None])
    back = lax.rem(cols - col + COLS, COLS)
    relay_row = jnp.sum(jnp.where(hit, back[None, None, :], 0), axis=2) * PLANES + cols[:, None]
    return send_pos, relay_row, land_row, own_source, own_rank, fits


def shards(
    blocks, pno_coef, source_dev, block_pos, pno_energy, occ_energy, pno_count, neighbour, coupling, intersection,
):
    me = lax.axis_index("pair")
    send_pos, relay_row, land_row, own_source, own_rank, fits = route(source_dev, block_pos, me)
    near = neighbour - (me - 1) * PAIRS
    table = jnp.concatenate([a.reshape(-1) for a in (send_pos, relay_row, land_row, near)])

    def finish(exchanging, source):
        return run_kernel(
            exchanging, table, pno_count, occ_energy, source, pno_coef, pno_energy, coupling, intersection
        )

    return lax.cond(
        fits,
        lambda: finish(True, blocks),
        lambda: finish(False, padded_exchange(blocks, pno_coef, send_pos, own_source, own_rank)),
    )


def solution(mesh):
    return jax.shard_map(
        shards,
        mesh=mesh,
        in_specs=(
            P("pair", "aux", None),
            P("pair", None, None),
            P(),
            P(),
            P("pair", None),
            P("pair"),
            P("pair"),
            P("pair", None),
            P("pair", None),
            P("pair", None, None, None),
        ),
        out_specs=(P("pair", None, None), P("pair")),
        check_vma=False,
    )
```

```python
import functools
import types

import jax
import jax.numpy as jnp
from jax import lax
from jax.experimental import pallas as pl
from jax.experimental.pallas import tpu as pltpu
from jax.sharding import PartitionSpec as P

ITERS = 3
MESH = pl.DeviceIdType.MESH

PLANES = 8
COLS = 8
OWNERS = PLANES * COLS
AUXES = 4
PAIRS = 16
REQ = 8
DOM = 4
BLOCKS = 64
TOTAL = PAIRS * REQ
TILE = 128
CAP = 3
DIRECT = 2
EXTRAS = (1, 2)

VMEM_LIMIT = 56 * 2**20
CHUNK = PAIRS // AUXES


def distance(step):
    dz, dy, _ = step
    return min(dz, PLANES - dz) + min(dy, 4 - dy)


STEPS = sorted(
    [(dz, dy, dc) for dz in range(PLANES) for dy in range(4) for dc in range(2) if (dz, dy, dc) != (0, 0, 0)],
    key=lambda s: -distance(s),
)


SCRATCH = {
    "inter": ((PAIRS, 4, TILE, TILE), jnp.float32),
    "vecs": ((PAIRS, TILE, 4 * TILE), jnp.bfloat16),
    "weighted": ((PAIRS, TILE, 4 * TILE), jnp.bfloat16),
    "window0": ((3 * PAIRS, TILE, TILE), jnp.bfloat16),
    "window1": ((3 * PAIRS, TILE, TILE), jnp.bfloat16),
    "window2": ((3 * PAIRS, TILE, TILE), jnp.bfloat16),
    "integ": ((PAIRS, TILE, TILE), jnp.float32),
    "inverse": ((PAIRS, TILE, TILE), jnp.float32),
    "own_part": ((CHUNK, TILE, TILE), jnp.float32),
    "share_out": ((AUXES - 1, CHUNK, TILE, TILE), jnp.bfloat16),
    "share_in": ((AUXES - 1, CHUNK, TILE, TILE), jnp.bfloat16),
    "high": ((PAIRS, TILE, TILE), jnp.bfloat16),
    "low": ((PAIRS, TILE, TILE), jnp.bfloat16),
    "local_sem": (2,),
    "x_send": (3, AUXES - 1),
    "x_recv": (3, AUXES - 1),
    "halo_send": (ITERS, 2),
    "halo_recv": (ITERS, 2),
}


def exchange_scratch(extra):
    return {
        "coef": ((PAIRS, DOM * TILE, TILE), jnp.bfloat16),
        "outgoing": ((DIRECT * OWNERS, TILE, TILE), jnp.bfloat16),
        "landing": ((DIRECT * OWNERS + extra * PLANES, TILE, TILE), jnp.bfloat16),
        "relay_out": ((OWNERS, TILE, TILE), jnp.bfloat16),
        "relay_in": ((OWNERS, TILE, TILE), jnp.bfloat16),
        "extra_out": ((extra * PLANES, TILE, TILE), jnp.bfloat16),
        "block_sem": (6,),
    }


SEND, RELAY, LAND = 0, OWNERS * CAP, OWNERS * CAP + PLANES * max(EXTRAS)
SUM, HIGH, LOW = range(3)


def kernel(extra, *refs):
    exchanging = extra > 0
    names = ["table", "count", "occ", "source", "coef_hbm", "energy", "near", "coupling", "inter_hbm", "amp", "pair_energy"]
    names += list(SCRATCH) + (list(exchange_scratch(extra)) if exchanging else [])
    if not exchanging:
        names.remove("coef_hbm")
    r = types.SimpleNamespace(**dict(zip(names, refs, strict=True)))
    me, ax = lax.axis_index("pair"), lax.axis_index("aux")
    plane, col = me // COLS, me % COLS
    y, core = col // 2, col % 2
    left, right = lax.rem(me + OWNERS - 1, OWNERS), lax.rem(me + 1, OWNERS)
    own = pl.multiple_of(ax * CHUNK, CHUNK)
    peers = [lax.rem(ax + k, AUXES) for k in range(AUXES)]
    windows = (r.window0, r.window1, r.window2)

    barrier = pltpu.get_barrier_semaphore()
    for k in range(1, AUXES):
        pl.semaphore_signal(barrier, inc=1, device_id=(me, peers[k]), device_id_type=MESH)
    if exchanging:

        def greet(k, carry):
            pl.semaphore_signal(barrier, inc=1, device_id=(lax.rem(me + k, OWNERS), ax), device_id_type=MESH)
            return carry

        lax.fori_loop(1, OWNERS, greet, 0)
        greeted = AUXES - 1 + OWNERS - 1
    else:
        for side in (left, right):
            pl.semaphore_signal(barrier, inc=1, device_id=(side, ax), device_id_type=MESH)
        greeted = AUXES - 1 + 2

    inter_copy = pltpu.make_async_copy(r.inter_hbm, r.inter, r.local_sem.at[0])
    if exchanging:
        coef_copy = pltpu.make_async_copy(r.coef_hbm, r.coef, r.local_sem.at[1])

    rows = lax.broadcasted_iota(jnp.int32, (TILE, TILE), 0)
    columns = lax.broadcasted_iota(jnp.int32, (TILE, TILE), 1)

    def masked(q, values):
        return jnp.where((rows < r.count[q]) & (columns < r.count[q]), values, 0.0)

    def prepare():
        def denominators(q, carry):
            across = jnp.broadcast_to(r.energy[pl.ds(q, 1), :], (TILE, TILE))
            r.inverse[q] = masked(q, 1.0 / (across + across.T + r.occ[q]))
            return carry

        lax.fori_loop(0, PAIRS, denominators, 0)
        inter_copy.wait()

        def narrow(q, carry):
            for n in range(4):
                v = r.inter[q, n]
                cut = slice(n * TILE, (n + 1) * TILE)
                r.vecs[q, :, cut] = v.astype(jnp.bfloat16)
                r.weighted[q, :, cut] = (v * r.coupling[n, q]).astype(jnp.bfloat16)
            return carry

        lax.fori_loop(0, PAIRS, narrow, 0)

    if exchanging:
        blocks, outgoing, landing = r.source, r.outgoing, r.landing

        def fill(k, carry):
            dst = lax.rem(me + k, OWNERS)
            for s in range(DIRECT):
                outgoing[DIRECT * k + s] = blocks[r.table[SEND + dst * CAP + s]]
            return carry

        def fill_relay(i, carry):
            k, b = i // PLANES, i % PLANES
            dst = b * COLS + lax.rem(col + k, COLS)
            r.relay_out[i] = blocks[r.table[SEND + dst * CAP + DIRECT]]
            return carry

        lax.fori_loop(0, OWNERS, fill, 0)
        lax.fori_loop(0, OWNERS, fill_relay, 0)
        for s in range(DIRECT):
            landing[s] = outgoing[s]
        for b in range(PLANES):
            r.relay_in[b] = r.relay_out[b]

        def whole(source, target, first, count, sem):
            return pltpu.make_async_remote_copy(
                src_ref=source.at[pl.ds(first, count)], dst_ref=target.at[pl.ds(first, count)],
                send_sem=r.block_sem.at[sem], recv_sem=r.block_sem.at[sem + 1],
                device_id=(right, ax), device_id_type=MESH,
            )

        def direct(dst):
            to, back = lax.rem(dst - me + OWNERS, OWNERS), lax.rem(me - dst + OWNERS, OWNERS)
            return pltpu.make_async_remote_copy(
                src_ref=outgoing.at[pl.ds(DIRECT * to, DIRECT)],
                dst_ref=landing.at[pl.ds(DIRECT * back, DIRECT)],
                send_sem=r.block_sem.at[0], recv_sem=r.block_sem.at[1],
                device_id=(dst, ax), device_id_type=MESH,
            )

        def to_relay(k):
            return pltpu.make_async_remote_copy(
                src_ref=r.relay_out.at[pl.ds(PLANES * k, PLANES)],
                dst_ref=r.relay_in.at[pl.ds(PLANES * (COLS - k), PLANES)],
                send_sem=r.block_sem.at[2], recv_sem=r.block_sem.at[3],
                device_id=(plane * COLS + lax.rem(col + k, COLS), ax), device_id_type=MESH,
            )

        def from_relay(k):
            return pltpu.make_async_remote_copy(
                src_ref=r.extra_out.at[pl.ds(extra * k, extra)],
                dst_ref=landing.at[pl.ds(DIRECT * OWNERS + extra * (PLANES - k), extra)],
                send_sem=r.block_sem.at[4], recv_sem=r.block_sem.at[5],
                device_id=(lax.rem(plane + k, PLANES) * COLS + col, ax), device_id_type=MESH,
            )

        pl.semaphore_wait(barrier, greeted)
        for k in range(1, COLS):
            to_relay(k).start()
        for dz, dy, dc in STEPS:
            direct(
                lax.rem(plane + dz, PLANES) * COLS + lax.rem(y + dy, 4) * 2 + lax.rem(core + dc, 2)
            ).start()
        inter_copy.start()
        coef_copy.start()
        prepare()

        relayed = whole(r.relay_out, r.relay_in, PLANES, PLANES * (COLS - 1), 2)
        relayed.wait_recv()
        for k in (4, 3, 5, 2, 6, 1, 7, 0):
            b = lax.rem(plane + k, PLANES)
            for e in range(extra):
                block = r.relay_in[r.table[RELAY + b * max(EXTRAS) + e]]
                if k == 0:
                    landing[DIRECT * OWNERS + e] = block
                else:
                    r.extra_out[extra * k + e] = block
            if k != 0:
                from_relay(k).start()

        coef_copy.wait()
        relayed.wait_send()
        sent = whole(outgoing, landing, DIRECT, DIRECT * (OWNERS - 1), 0)
        sent.wait_send()
        sent.wait_recv()
        extras = pltpu.make_async_remote_copy(
            src_ref=r.extra_out.at[pl.ds(extra, extra * (PLANES - 1))],
            dst_ref=landing.at[pl.ds(DIRECT * OWNERS + extra, extra * (PLANES - 1))],
            send_sem=r.block_sem.at[4], recv_sem=r.block_sem.at[5],
            device_id=(right, ax), device_id_type=MESH,
        )
        extras.wait_send()
        extras.wait_recv()

        def part(q):
            rows_of = [
                jnp.concatenate(
                    [landing[r.table[LAND + q * REQ + m * DOM + t]] for t in range(DOM)], axis=1
                )
                for m in range(2)
            ]
            projected = jnp.dot(
                jnp.concatenate(rows_of, axis=0), r.coef[q], preferred_element_type=jnp.float32
            ).astype(jnp.bfloat16)
            return lax.dot_general(
                projected[:TILE], projected[TILE:], (((0,), (0,)), ((), ())),
                preferred_element_type=jnp.float32,
            )

    else:
        inter_copy.start()
        prepare()
        pl.semaphore_wait(barrier, greeted)

        def part(q):
            return r.source[q]

    def share(k):
        return pltpu.make_async_remote_copy(
            src_ref=r.share_out.at[k - 1], dst_ref=r.share_in.at[AUXES - 1 - k],
            send_sem=r.x_send.at[SUM, k - 1], recv_sem=r.x_recv.at[SUM, AUXES - 1 - k],
            device_id=(me, peers[k]), device_id_type=MESH,
        )

    def spread(kind, k):
        values = r.high if kind == HIGH else r.low
        return pltpu.make_async_remote_copy(
            src_ref=values.at[pl.ds(own, CHUNK)], dst_ref=values.at[pl.ds(own, CHUNK)],
            send_sem=r.x_send.at[kind, k - 1], recv_sem=r.x_recv.at[kind, AUXES - 1 - k],
            device_id=(me, peers[k]), device_id_type=MESH,
        )

    def wait_shares():
        for k in range(1, AUXES):
            pltpu.make_async_remote_copy(
                src_ref=r.share_in.at[k - 1], dst_ref=r.share_in.at[k - 1],
                send_sem=r.x_send.at[SUM, k - 1], recv_sem=r.x_recv.at[SUM, k - 1],
                device_id=(me, peers[k]), device_id_type=MESH,
            ).wait_recv()

    def wait_spread(kind, k):
        values = r.high if kind == HIGH else r.low
        theirs = values.at[pl.ds(peers[k] * CHUNK, CHUNK)]
        pltpu.make_async_remote_copy(
            src_ref=theirs, dst_ref=theirs,
            send_sem=r.x_send.at[kind, k - 1], recv_sem=r.x_recv.at[kind, k - 1],
            device_id=(me, peers[k]), device_id_type=MESH,
        ).wait_recv()

    def halo(sweep, first, size, side):
        target = first + 2 * PAIRS if side == 0 else first
        return pltpu.make_async_remote_copy(
            src_ref=windows[sweep].at[pl.ds(PAIRS + first, size)],
            dst_ref=windows[sweep].at[pl.ds(target, size)],
            send_sem=r.halo_send.at[sweep, side], recv_sem=r.halo_recv.at[sweep, side],
            device_id=(left if side == 0 else right, ax), device_id_type=MESH,
        )

    def wait_halo(sweep):
        for side in range(2):
            done = pltpu.make_async_remote_copy(
                src_ref=windows[sweep].at[pl.ds(PAIRS, PAIRS)],
                dst_ref=windows[sweep].at[pl.ds(2 * PAIRS if side == 0 else 0, PAIRS)],
                send_sem=r.halo_send.at[sweep, side], recv_sem=r.halo_recv.at[sweep, side],
                device_id=(left if side == 0 else right, ax), device_id_type=MESH,
            )
            done.wait_send()
            done.wait_recv()

    for k in (2, 1, 3):
        for i in range(CHUNK):
            r.share_out[k - 1, i] = part(peers[k] * CHUNK + i).astype(jnp.bfloat16)
        share(k).start()
    for i in range(CHUNK):
        r.own_part[i] = part(own + i)
    wait_shares()

    def add(i, carry):
        values = r.own_part[i]
        for k in range(AUXES - 1):
            values = values + r.share_in[k, i].astype(jnp.float32)
        values = masked(own + i, values)
        top = values.astype(jnp.bfloat16)
        r.high[own + i] = top
        r.low[own + i] = (values - top.astype(jnp.float32)).astype(jnp.bfloat16)
        return carry

    lax.fori_loop(0, CHUNK, add, 0)
    for kind in (HIGH, LOW):
        for k in (2, 1, 3):
            spread(kind, k).start()

    def first_amplitudes(start):
        def body(i, carry):
            q = start + i
            windows[0][PAIRS + q] = (-r.high[q].astype(jnp.float32) * r.inverse[q]).astype(jnp.bfloat16)
            return carry

        lax.fori_loop(0, CHUNK, body, 0)
        for side in range(2):
            halo(0, start, CHUNK, side).start()

    first_amplitudes(own)
    for k in (1, 3, 2):
        wait_spread(HIGH, k)
        first_amplitudes(pl.multiple_of(peers[k] * CHUNK, CHUNK))

    for sweep in range(ITERS):
        wait_halo(sweep)
        if sweep == 0:
            for k in (1, 3, 2):
                wait_spread(LOW, k)

        def update(q, sweep=sweep):
            firsts = [
                jnp.dot(
                    r.weighted[q, :, n * TILE : (n + 1) * TILE],
                    windows[sweep][jnp.clip(r.near[n, q] - (me - 1) * PAIRS, 0, 3 * PAIRS - 1)],
                    preferred_element_type=jnp.float32,
                ).astype(jnp.bfloat16)
                for n in range(4)
            ]
            coupled = lax.dot_general(
                jnp.concatenate(firsts, axis=1), r.vecs[q], (((1,), (1,)), ((), ())),
                preferred_element_type=jnp.float32,
            )
            if sweep == 0:
                integrals = r.high[q].astype(jnp.float32) + r.low[q].astype(jnp.float32)
                r.integ[q] = integrals
            else:
                integrals = r.integ[q]
            current = (coupled - integrals) * r.inverse[q]
            if sweep < ITERS - 1:
                windows[sweep + 1][PAIRS + q] = current.astype(jnp.bfloat16)
            else:
                r.amp[q] = current
                r.pair_energy[q] = jnp.sum(integrals * (2.0 * current - current.T))

        def some(j, carry, sweep=sweep):
            for i in range(CHUNK):
                update(j * CHUNK + i)
            if sweep < ITERS - 1:
                for side in range(2):
                    halo(sweep + 1, pl.multiple_of(j * CHUNK, CHUNK), CHUNK, side).start()
            return carry

        lax.fori_loop(0, PAIRS // CHUNK, some, 0)

    for k in range(1, AUXES):
        share(k).wait_send()
        for kind in (HIGH, LOW):
            spread(kind, k).wait_send()


def run_kernel(extra, table, count, occ, source, coef, energy, near, coupling, inter):
    exchanging = extra > 0
    smem, vmem = pl.BlockSpec(memory_space=pltpu.SMEM), pl.BlockSpec(memory_space=pltpu.VMEM)
    hbm = pl.BlockSpec(memory_space=pl.ANY)
    scratch = dict(SCRATCH, **(exchange_scratch(extra) if exchanging else {}))
    return pl.pallas_call(
        functools.partial(kernel, extra),
        out_shape=(
            jax.ShapeDtypeStruct((PAIRS, TILE, TILE), jnp.float32),
            jax.ShapeDtypeStruct((PAIRS,), jnp.float32),
        ),
        in_specs=[smem, smem, smem, vmem] + [hbm] * exchanging + [vmem, smem, smem, hbm],
        out_specs=(vmem, smem),
        scratch_shapes=[
            pltpu.SemaphoreType.DMA(v) if isinstance(v[0], int) else pltpu.VMEM(*v) for v in scratch.values()
        ],
        compiler_params=pltpu.CompilerParams(
            collective_id=extra, has_side_effects=True, vmem_limit_bytes=VMEM_LIMIT
        ),
    )(*([table, count, occ, source] + [coef] * exchanging + [energy, near, coupling, inter]))


def padded_exchange(blocks, coef, send_pos, own_source, own_rank):
    incoming = lax.all_to_all(
        blocks[send_pos], "pair", split_axis=0, concat_axis=0, tiled=True
    )
    arrived = incoming.reshape((OWNERS * CAP,) + blocks.shape[1:])[own_source * CAP + own_rank]
    arrived = arrived.reshape((PAIRS, 2, DOM) + blocks.shape[1:])
    coefs = coef.reshape(PAIRS, DOM, TILE, TILE)
    projected = jnp.einsum(
        "qmtxp,qtpn->qmxn", arrived, coefs, preferred_element_type=jnp.float32
    ).astype(jnp.bfloat16)
    return jnp.einsum(
        "qxa,qxb->qab", projected[:, 0], projected[:, 1], preferred_element_type=jnp.float32
    )


def route(source_dev, block_pos, me):
    plane, col = me // COLS, me % COLS
    both = (source_dev * BLOCKS + block_pos).reshape(OWNERS, TOTAL)
    source, position = both // BLOCKS, both % BLOCKS
    slots = jnp.arange(CAP, dtype=jnp.int32)
    devices = jnp.arange(OWNERS, dtype=jnp.int32)
    wanted = source == me
    ranking = jnp.cumsum(wanted.astype(jnp.int32), axis=1) - 1
    chosen = wanted[:, None, :] & (ranking[:, None, :] == slots[None, :, None])
    send_pos = jnp.sum(jnp.where(chosen, position[:, None, :], 0), axis=2)
    taken = jnp.sum((source[:, None, :] == devices[None, :, None]).astype(jnp.int32), axis=2)
    third = (taken > DIRECT).astype(jnp.int32)
    most = jnp.max(jnp.sum(third.reshape(OWNERS, PLANES, COLS), axis=2))
    room = jnp.minimum(jnp.maximum(most, EXTRAS[0]), EXTRAS[1])
    own_source = lax.dynamic_index_in_dim(source, me, 0, keepdims=False)
    order = jnp.arange(TOTAL, dtype=jnp.int32)
    earlier = (own_source[None, :] == own_source[:, None]) & (order[None, :] < order[:, None])
    own_rank = jnp.sum(earlier.astype(jnp.int32), axis=1)
    own_third = lax.dynamic_index_in_dim(third, me, 0, keepdims=False)
    before = (devices[None, :] < own_source[:, None]) & (
        devices[None, :] // COLS == own_source[:, None] // COLS
    )
    extra_rank = jnp.sum(jnp.where(before, own_third[None, :], 0), axis=1)
    extra_row = (
        DIRECT * OWNERS
        + lax.rem(own_source // COLS - plane + PLANES, PLANES) * room
        + jnp.minimum(extra_rank, room - 1)
    )
    direct_row = lax.rem(own_source - me + OWNERS, OWNERS) * DIRECT + own_rank
    land_row = jnp.where(own_rank >= DIRECT, extra_row, direct_row)
    column = lax.dynamic_index_in_dim(third.reshape(PLANES, COLS, PLANES, COLS), col, 1, keepdims=False)
    column = lax.dynamic_index_in_dim(column, plane, 1, keepdims=False)
    cols = jnp.arange(COLS, dtype=jnp.int32)
    place = jnp.cumsum(column, axis=1) - column
    hit = (column == 1)[:, None, :] & (place[:, None, :] == jnp.arange(EXTRAS[1])[None, :, None])
    back = lax.rem(cols - col + COLS, COLS)
    relay_row = jnp.sum(jnp.where(hit, back[None, None, :], 0), axis=2) * PLANES + cols[:, None]
    return send_pos, relay_row, land_row, own_source, own_rank, most


def shards(
    blocks, pno_coef, source_dev, block_pos, pno_energy, occ_energy, pno_count, neighbour, coupling, intersection,
):
    me = lax.axis_index("pair")
    send_pos, relay_row, land_row, own_source, own_rank, most = route(source_dev, block_pos, me)
    table = jnp.concatenate([a.reshape(-1) for a in (send_pos, relay_row, land_row)])

    def finish(extra, source):
        return run_kernel(
            extra, table, pno_count, occ_energy, source, pno_coef, pno_energy, neighbour.T, coupling.T, intersection
        )

    return lax.switch(
        jnp.clip(most, 1, 3) - 1,
        [
            lambda: finish(1, blocks),
            lambda: finish(2, blocks),
            lambda: finish(0, padded_exchange(blocks, pno_coef, send_pos, own_source, own_rank)),
        ],
    )


def solution(mesh):
    return jax.shard_map(
        shards,
        mesh=mesh,
        in_specs=(
            P("pair", "aux", None),
            P("pair", None, None),
            P(),
            P(),
            P("pair", None),
            P("pair"),
            P("pair"),
            P("pair", None),
            P("pair", None),
            P("pair", None, None, None),
        ),
        out_specs=(P("pair", None, None), P("pair")),
        check_vma=False,
    )
```

```python
import functools
import types

import jax
import jax.numpy as jnp
from jax import lax
from jax.experimental import pallas as pl
from jax.experimental.pallas import tpu as pltpu
from jax.sharding import PartitionSpec as P

ITERS = 3
MESH = pl.DeviceIdType.MESH

PLANES = 8
COLS = 8
OWNERS = PLANES * COLS
AUXES = 4
PAIRS = 16
REQ = 8
DOM = 4
BLOCKS = 64
TOTAL = PAIRS * REQ
TILE = 128
CAP = 3
DIRECT = 2
EXTRAS = (1, 2)

VMEM_LIMIT = 56 * 2**20
CHUNK = PAIRS // AUXES


def distance(step):
    dz, dy, _ = step
    return min(dz, PLANES - dz) + min(dy, 4 - dy)


STEPS = sorted(
    [(dz, dy, dc) for dz in range(PLANES) for dy in range(4) for dc in range(2) if (dz, dy, dc) != (0, 0, 0)],
    key=lambda s: -distance(s),
)


SCRATCH = {
    "inter": ((PAIRS, 4, TILE, TILE), jnp.float32),
    "vecs": ((PAIRS, TILE, 4 * TILE), jnp.bfloat16),
    "weighted": ((PAIRS, TILE, 4 * TILE), jnp.bfloat16),
    "window0": ((3 * PAIRS, TILE, TILE), jnp.bfloat16),
    "window1": ((3 * PAIRS, TILE, TILE), jnp.bfloat16),
    "window2": ((3 * PAIRS, TILE, TILE), jnp.bfloat16),
    "inverse": ((PAIRS, TILE, TILE), jnp.float32),
    "integ": ((PAIRS, TILE, TILE), jnp.float32),
    "factor": ((PAIRS, TILE, TILE), jnp.float32),
    "own_part": ((CHUNK, TILE, TILE), jnp.float32),
    "share_out": ((AUXES - 1, CHUNK, TILE, TILE), jnp.bfloat16),
    "share_in": ((AUXES - 1, CHUNK, TILE, TILE), jnp.bfloat16),
    "high": ((PAIRS, TILE, TILE), jnp.bfloat16),
    "low": ((PAIRS, TILE, TILE), jnp.bfloat16),
    "local_sem": (2,),
    "x_send": (3, AUXES - 1),
    "x_recv": (3, AUXES - 1),
    "halo_send": (ITERS, 2),
    "halo_recv": (ITERS, 2),
}


def exchange_scratch(extra):
    return {
        "coef": ((PAIRS, DOM * TILE, TILE), jnp.bfloat16),
        "outgoing": ((DIRECT * OWNERS, TILE, TILE), jnp.bfloat16),
        "landing": ((DIRECT * OWNERS + extra * PLANES, TILE, TILE), jnp.bfloat16),
        "relay_out": ((OWNERS, TILE, TILE), jnp.bfloat16),
        "relay_in": ((OWNERS, TILE, TILE), jnp.bfloat16),
        "extra_out": ((extra * PLANES, TILE, TILE), jnp.bfloat16),
        "block_sem": (6,),
    }


SEND, RELAY, LAND = 0, OWNERS * CAP, OWNERS * CAP + PLANES * max(EXTRAS)
SUM, HIGH, LOW = range(3)


def kernel(extra, *refs):
    exchanging = extra > 0
    names = ["table", "count", "occ", "source", "coef_hbm", "energy", "near", "coupling", "inter_hbm", "amp", "pair_energy"]
    names += list(SCRATCH) + (list(exchange_scratch(extra)) if exchanging else [])
    if not exchanging:
        names.remove("coef_hbm")
    r = types.SimpleNamespace(**dict(zip(names, refs, strict=True)))
    me, ax = lax.axis_index("pair"), lax.axis_index("aux")
    plane, col = me // COLS, me % COLS
    y, core = col // 2, col % 2
    left, right = lax.rem(me + OWNERS - 1, OWNERS), lax.rem(me + 1, OWNERS)
    own = pl.multiple_of(ax * CHUNK, CHUNK)
    peers = [lax.rem(ax + k, AUXES) for k in range(AUXES)]
    windows = (r.window0, r.window1, r.window2)

    barrier = pltpu.get_barrier_semaphore()
    for k in range(1, AUXES):
        pl.semaphore_signal(barrier, inc=1, device_id=(me, peers[k]), device_id_type=MESH)
    if exchanging:

        def greet(k, carry):
            pl.semaphore_signal(barrier, inc=1, device_id=(lax.rem(me + k, OWNERS), ax), device_id_type=MESH)
            return carry

        lax.fori_loop(1, OWNERS, greet, 0)
        greeted = AUXES - 1 + OWNERS - 1
    else:
        for side in (left, right):
            pl.semaphore_signal(barrier, inc=1, device_id=(side, ax), device_id_type=MESH)
        greeted = AUXES - 1 + 2

    inter_copy = pltpu.make_async_copy(r.inter_hbm, r.inter, r.local_sem.at[0])
    if exchanging:
        coef_copy = pltpu.make_async_copy(r.coef_hbm, r.coef, r.local_sem.at[1])

    rows = lax.broadcasted_iota(jnp.int32, (TILE, TILE), 0)
    columns = lax.broadcasted_iota(jnp.int32, (TILE, TILE), 1)

    def masked(q, values):
        return jnp.where((rows < r.count[q]) & (columns < r.count[q]), values, 0.0)

    def prepare():
        def denominators(q, carry):
            across = jnp.broadcast_to(r.energy[pl.ds(q, 1), :], (TILE, TILE))
            r.inverse[q] = masked(q, 1.0 / (across + across.T + r.occ[q]))
            return carry

        lax.fori_loop(0, PAIRS, denominators, 0)
        inter_copy.wait()

        def narrow(q, carry):
            for n in range(4):
                v = r.inter[q, n]
                cut = slice(n * TILE, (n + 1) * TILE)
                r.vecs[q, :, cut] = v.astype(jnp.bfloat16)
                r.weighted[q, :, cut] = (v * r.coupling[n, q]).astype(jnp.bfloat16)
            return carry

        lax.fori_loop(0, PAIRS, narrow, 0)

    if exchanging:
        blocks, outgoing, landing = r.source, r.outgoing, r.landing

        def fill(k, carry):
            dst = lax.rem(me + k, OWNERS)
            for s in range(DIRECT):
                outgoing[DIRECT * k + s] = blocks[r.table[SEND + dst * CAP + s]]
            return carry

        def fill_relay(i, carry):
            k, b = i // PLANES, i % PLANES
            dst = b * COLS + lax.rem(col + k, COLS)
            r.relay_out[i] = blocks[r.table[SEND + dst * CAP + DIRECT]]
            return carry

        lax.fori_loop(0, OWNERS, fill, 0)
        lax.fori_loop(0, OWNERS, fill_relay, 0)
        for s in range(DIRECT):
            landing[s] = outgoing[s]
        for b in range(PLANES):
            r.relay_in[b] = r.relay_out[b]

        def whole(source, target, first, count, sem):
            return pltpu.make_async_remote_copy(
                src_ref=source.at[pl.ds(first, count)], dst_ref=target.at[pl.ds(first, count)],
                send_sem=r.block_sem.at[sem], recv_sem=r.block_sem.at[sem + 1],
                device_id=(right, ax), device_id_type=MESH,
            )

        def direct(dst):
            to, back = lax.rem(dst - me + OWNERS, OWNERS), lax.rem(me - dst + OWNERS, OWNERS)
            return pltpu.make_async_remote_copy(
                src_ref=outgoing.at[pl.ds(DIRECT * to, DIRECT)],
                dst_ref=landing.at[pl.ds(DIRECT * back, DIRECT)],
                send_sem=r.block_sem.at[0], recv_sem=r.block_sem.at[1],
                device_id=(dst, ax), device_id_type=MESH,
            )

        def to_relay(k):
            return pltpu.make_async_remote_copy(
                src_ref=r.relay_out.at[pl.ds(PLANES * k, PLANES)],
                dst_ref=r.relay_in.at[pl.ds(PLANES * (COLS - k), PLANES)],
                send_sem=r.block_sem.at[2], recv_sem=r.block_sem.at[3],
                device_id=(plane * COLS + lax.rem(col + k, COLS), ax), device_id_type=MESH,
            )

        def from_relay(k):
            return pltpu.make_async_remote_copy(
                src_ref=r.extra_out.at[pl.ds(extra * k, extra)],
                dst_ref=landing.at[pl.ds(DIRECT * OWNERS + extra * (PLANES - k), extra)],
                send_sem=r.block_sem.at[4], recv_sem=r.block_sem.at[5],
                device_id=(lax.rem(plane + k, PLANES) * COLS + col, ax), device_id_type=MESH,
            )

        pl.semaphore_wait(barrier, greeted)
        for k in range(1, COLS):
            to_relay(k).start()
        for dz, dy, dc in STEPS:
            direct(
                lax.rem(plane + dz, PLANES) * COLS + lax.rem(y + dy, 4) * 2 + lax.rem(core + dc, 2)
            ).start()
        inter_copy.start()
        coef_copy.start()
        prepare()

        relayed = whole(r.relay_out, r.relay_in, PLANES, PLANES * (COLS - 1), 2)
        relayed.wait_recv()
        for k in (4, 3, 5, 2, 6, 1, 7, 0):
            b = lax.rem(plane + k, PLANES)
            for e in range(extra):
                block = r.relay_in[r.table[RELAY + b * max(EXTRAS) + e]]
                if k == 0:
                    landing[DIRECT * OWNERS + e] = block
                else:
                    r.extra_out[extra * k + e] = block
            if k != 0:
                from_relay(k).start()

        coef_copy.wait()
        relayed.wait_send()
        sent = whole(outgoing, landing, DIRECT, DIRECT * (OWNERS - 1), 0)
        sent.wait_send()
        sent.wait_recv()
        extras = pltpu.make_async_remote_copy(
            src_ref=r.extra_out.at[pl.ds(extra, extra * (PLANES - 1))],
            dst_ref=landing.at[pl.ds(DIRECT * OWNERS + extra, extra * (PLANES - 1))],
            send_sem=r.block_sem.at[4], recv_sem=r.block_sem.at[5],
            device_id=(right, ax), device_id_type=MESH,
        )
        extras.wait_send()
        extras.wait_recv()

        def part(q):
            rows_of = [
                jnp.concatenate(
                    [landing[r.table[LAND + q * REQ + m * DOM + t]] for t in range(DOM)], axis=1
                )
                for m in range(2)
            ]
            projected = jnp.dot(
                jnp.concatenate(rows_of, axis=0), r.coef[q], preferred_element_type=jnp.float32
            ).astype(jnp.bfloat16)
            return lax.dot_general(
                projected[:TILE], projected[TILE:], (((0,), (0,)), ((), ())),
                preferred_element_type=jnp.float32,
            )

    else:
        inter_copy.start()
        prepare()
        pl.semaphore_wait(barrier, greeted)

        def part(q):
            return r.source[q]

    def share(k):
        return pltpu.make_async_remote_copy(
            src_ref=r.share_out.at[k - 1], dst_ref=r.share_in.at[AUXES - 1 - k],
            send_sem=r.x_send.at[SUM, k - 1], recv_sem=r.x_recv.at[SUM, AUXES - 1 - k],
            device_id=(me, peers[k]), device_id_type=MESH,
        )

    def spread(kind, k):
        values = r.high if kind == HIGH else r.low
        return pltpu.make_async_remote_copy(
            src_ref=values.at[pl.ds(own, CHUNK)], dst_ref=values.at[pl.ds(own, CHUNK)],
            send_sem=r.x_send.at[kind, k - 1], recv_sem=r.x_recv.at[kind, AUXES - 1 - k],
            device_id=(me, peers[k]), device_id_type=MESH,
        )

    def wait_shares():
        for k in range(1, AUXES):
            pltpu.make_async_remote_copy(
                src_ref=r.share_in.at[k - 1], dst_ref=r.share_in.at[k - 1],
                send_sem=r.x_send.at[SUM, k - 1], recv_sem=r.x_recv.at[SUM, k - 1],
                device_id=(me, peers[k]), device_id_type=MESH,
            ).wait_recv()

    def wait_spread(kind, k):
        values = r.high if kind == HIGH else r.low
        theirs = values.at[pl.ds(peers[k] * CHUNK, CHUNK)]
        pltpu.make_async_remote_copy(
            src_ref=theirs, dst_ref=theirs,
            send_sem=r.x_send.at[kind, k - 1], recv_sem=r.x_recv.at[kind, k - 1],
            device_id=(me, peers[k]), device_id_type=MESH,
        ).wait_recv()

    def halo(sweep, first, size, side):
        target = first + 2 * PAIRS if side == 0 else first
        return pltpu.make_async_remote_copy(
            src_ref=windows[sweep].at[pl.ds(PAIRS + first, size)],
            dst_ref=windows[sweep].at[pl.ds(target, size)],
            send_sem=r.halo_send.at[sweep, side], recv_sem=r.halo_recv.at[sweep, side],
            device_id=(left if side == 0 else right, ax), device_id_type=MESH,
        )

    def wait_halo(sweep):
        for side in range(2):
            done = pltpu.make_async_remote_copy(
                src_ref=windows[sweep].at[pl.ds(PAIRS, PAIRS)],
                dst_ref=windows[sweep].at[pl.ds(2 * PAIRS if side == 0 else 0, PAIRS)],
                send_sem=r.halo_send.at[sweep, side], recv_sem=r.halo_recv.at[sweep, side],
                device_id=(left if side == 0 else right, ax), device_id_type=MESH,
            )
            done.wait_send()
            done.wait_recv()

    for k in (2, 1, 3):
        for i in range(CHUNK):
            r.share_out[k - 1, i] = part(peers[k] * CHUNK + i).astype(jnp.bfloat16)
        share(k).start()
    for i in range(CHUNK):
        r.own_part[i] = part(own + i)
    wait_shares()

    def add(i, carry):
        values = r.own_part[i]
        for k in range(AUXES - 1):
            values = values + r.share_in[k, i].astype(jnp.float32)
        values = masked(own + i, values)
        top = values.astype(jnp.bfloat16)
        r.high[own + i] = top
        r.low[own + i] = (values - top.astype(jnp.float32)).astype(jnp.bfloat16)
        return carry

    lax.fori_loop(0, CHUNK, add, 0)
    for k in (2, 1, 3):
        spread(HIGH, k).start()

    def first_amplitudes(start):
        def body(i, carry):
            q = start + i
            windows[0][PAIRS + q] = (-r.high[q].astype(jnp.float32) * r.inverse[q]).astype(jnp.bfloat16)
            return carry

        lax.fori_loop(0, CHUNK, body, 0)
        for side in range(2):
            halo(0, start, CHUNK, side).start()

    first_amplitudes(own)
    for k in (1, 3, 2):
        wait_spread(HIGH, k)
        first_amplitudes(pl.multiple_of(peers[k] * CHUNK, CHUNK))
    for k in (2, 1, 3):
        spread(LOW, k).start()

    def both_halves(q, carry):
        integrals = r.high[q].astype(jnp.float32) + r.low[q].astype(jnp.float32)
        r.integ[q] = integrals
        r.factor[q] = 2.0 * integrals - integrals.T
        return carry

    for sweep in range(ITERS):
        if sweep == ITERS - 1:
            for k in (1, 3, 2):
                wait_spread(LOW, k)
            lax.fori_loop(0, PAIRS, both_halves, 0)
        wait_halo(sweep)

        def update(q, sweep=sweep):
            firsts = [
                jnp.dot(
                    r.weighted[q, :, n * TILE : (n + 1) * TILE],
                    windows[sweep][jnp.clip(r.near[n, q] - (me - 1) * PAIRS, 0, 3 * PAIRS - 1)],
                    preferred_element_type=jnp.float32,
                ).astype(jnp.bfloat16)
                for n in range(4)
            ]
            coupled = lax.dot_general(
                jnp.concatenate(firsts, axis=1), r.vecs[q], (((1,), (1,)), ((), ())),
                preferred_element_type=jnp.float32,
            )
            integrals = r.high[q].astype(jnp.float32) if sweep < ITERS - 1 else r.integ[q]
            current = (coupled - integrals) * r.inverse[q]
            if sweep < ITERS - 1:
                windows[sweep + 1][PAIRS + q] = current.astype(jnp.bfloat16)
            else:
                r.amp[q] = current
                r.pair_energy[q] = jnp.sum(r.factor[q] * current)

        def some(j, carry, sweep=sweep):
            for i in range(CHUNK):
                update(j * CHUNK + i)
            if sweep < ITERS - 1:
                for side in range(2):
                    halo(sweep + 1, pl.multiple_of(j * CHUNK, CHUNK), CHUNK, side).start()
            return carry

        lax.fori_loop(0, PAIRS // CHUNK, some, 0)

    for k in range(1, AUXES):
        share(k).wait_send()
        for kind in (HIGH, LOW):
            spread(kind, k).wait_send()


def run_kernel(extra, table, count, occ, source, coef, energy, near, coupling, inter):
    exchanging = extra > 0
    smem, vmem = pl.BlockSpec(memory_space=pltpu.SMEM), pl.BlockSpec(memory_space=pltpu.VMEM)
    hbm = pl.BlockSpec(memory_space=pl.ANY)
    scratch = dict(SCRATCH, **(exchange_scratch(extra) if exchanging else {}))
    return pl.pallas_call(
        functools.partial(kernel, extra),
        out_shape=(
            jax.ShapeDtypeStruct((PAIRS, TILE, TILE), jnp.float32),
            jax.ShapeDtypeStruct((PAIRS,), jnp.float32),
        ),
        in_specs=[smem, smem, smem, vmem] + [hbm] * exchanging + [vmem, smem, smem, hbm],
        out_specs=(vmem, smem),
        scratch_shapes=[
            pltpu.SemaphoreType.DMA(v) if isinstance(v[0], int) else pltpu.VMEM(*v) for v in scratch.values()
        ],
        compiler_params=pltpu.CompilerParams(
            collective_id=extra, has_side_effects=True, vmem_limit_bytes=VMEM_LIMIT
        ),
    )(*([table, count, occ, source] + [coef] * exchanging + [energy, near, coupling, inter]))


def padded_exchange(blocks, coef, send_pos, own_source, own_rank):
    incoming = lax.all_to_all(
        blocks[send_pos], "pair", split_axis=0, concat_axis=0, tiled=True
    )
    arrived = incoming.reshape((OWNERS * CAP,) + blocks.shape[1:])[own_source * CAP + own_rank]
    arrived = arrived.reshape((PAIRS, 2, DOM) + blocks.shape[1:])
    coefs = coef.reshape(PAIRS, DOM, TILE, TILE)
    projected = jnp.einsum(
        "qmtxp,qtpn->qmxn", arrived, coefs, preferred_element_type=jnp.float32
    ).astype(jnp.bfloat16)
    return jnp.einsum(
        "qxa,qxb->qab", projected[:, 0], projected[:, 1], preferred_element_type=jnp.float32
    )


def route(source_dev, block_pos, me):
    plane, col = me // COLS, me % COLS
    both = (source_dev * BLOCKS + block_pos).reshape(OWNERS, TOTAL)
    source, position = both // BLOCKS, both % BLOCKS
    slots = jnp.arange(CAP, dtype=jnp.int32)
    devices = jnp.arange(OWNERS, dtype=jnp.int32)
    wanted = source == me
    ranking = jnp.cumsum(wanted.astype(jnp.int32), axis=1) - 1
    chosen = wanted[:, None, :] & (ranking[:, None, :] == slots[None, :, None])
    send_pos = jnp.sum(jnp.where(chosen, position[:, None, :], 0), axis=2)
    taken = jnp.sum((source[:, None, :] == devices[None, :, None]).astype(jnp.int32), axis=2)
    third = (taken > DIRECT).astype(jnp.int32)
    most = jnp.max(jnp.sum(third.reshape(OWNERS, PLANES, COLS), axis=2))
    room = jnp.minimum(jnp.maximum(most, EXTRAS[0]), EXTRAS[1])
    own_source = lax.dynamic_index_in_dim(source, me, 0, keepdims=False)
    order = jnp.arange(TOTAL, dtype=jnp.int32)
    earlier = (own_source[None, :] == own_source[:, None]) & (order[None, :] < order[:, None])
    own_rank = jnp.sum(earlier.astype(jnp.int32), axis=1)
    own_third = lax.dynamic_index_in_dim(third, me, 0, keepdims=False)
    before = (devices[None, :] < own_source[:, None]) & (
        devices[None, :] // COLS == own_source[:, None] // COLS
    )
    extra_rank = jnp.sum(jnp.where(before, own_third[None, :], 0), axis=1)
    extra_row = (
        DIRECT * OWNERS
        + lax.rem(own_source // COLS - plane + PLANES, PLANES) * room
        + jnp.minimum(extra_rank, room - 1)
    )
    direct_row = lax.rem(own_source - me + OWNERS, OWNERS) * DIRECT + own_rank
    land_row = jnp.where(own_rank >= DIRECT, extra_row, direct_row)
    column = lax.dynamic_index_in_dim(third.reshape(PLANES, COLS, PLANES, COLS), col, 1, keepdims=False)
    column = lax.dynamic_index_in_dim(column, plane, 1, keepdims=False)
    cols = jnp.arange(COLS, dtype=jnp.int32)
    place = jnp.cumsum(column, axis=1) - column
    hit = (column == 1)[:, None, :] & (place[:, None, :] == jnp.arange(EXTRAS[1])[None, :, None])
    back = lax.rem(cols - col + COLS, COLS)
    relay_row = jnp.sum(jnp.where(hit, back[None, None, :], 0), axis=2) * PLANES + cols[:, None]
    return send_pos, relay_row, land_row, own_source, own_rank, most


def shards(
    blocks, pno_coef, source_dev, block_pos, pno_energy, occ_energy, pno_count, neighbour, coupling, intersection,
):
    me = lax.axis_index("pair")
    send_pos, relay_row, land_row, own_source, own_rank, most = route(source_dev, block_pos, me)
    table = jnp.concatenate([a.reshape(-1) for a in (send_pos, relay_row, land_row)])

    def finish(extra, source):
        return run_kernel(
            extra, table, pno_count, occ_energy, source, pno_coef, pno_energy, neighbour.T, coupling.T, intersection
        )

    return lax.switch(
        jnp.clip(most, 1, 3) - 1,
        [
            lambda: finish(1, blocks),
            lambda: finish(2, blocks),
            lambda: finish(0, padded_exchange(blocks, pno_coef, send_pos, own_source, own_rank)),
        ],
    )


def solution(mesh):
    return jax.shard_map(
        shards,
        mesh=mesh,
        in_specs=(
            P("pair", "aux", None),
            P("pair", None, None),
            P(),
            P(),
            P("pair", None),
            P("pair"),
            P("pair"),
            P("pair", None),
            P("pair", None),
            P("pair", None, None, None),
        ),
        out_specs=(P("pair", None, None), P("pair")),
        check_vma=False,
    )
```

```python
import functools
import types

import jax
import jax.numpy as jnp
from jax import lax
from jax.experimental import pallas as pl
from jax.experimental.pallas import tpu as pltpu
from jax.sharding import PartitionSpec as P

ITERS = 3
MESH = pl.DeviceIdType.MESH

PLANES = 8
COLS = 8
OWNERS = PLANES * COLS
AUXES = 4
PAIRS = 16
REQ = 8
DOM = 4
BLOCKS = 64
TOTAL = PAIRS * REQ
TILE = 128
CAP = 3
DIRECT = 2
EXTRAS = (1, 2)

VMEM_LIMIT = 56 * 2**20
CHUNK = PAIRS // AUXES


def distance(step):
    dz, dy, _ = step
    return min(dz, PLANES - dz) + min(dy, 4 - dy)


STEPS = sorted(
    [(dz, dy, dc) for dz in range(PLANES) for dy in range(4) for dc in range(2) if (dz, dy, dc) != (0, 0, 0)],
    key=lambda s: -distance(s),
)


SCRATCH = {
    "inter": ((PAIRS, 4, TILE, TILE), jnp.float32),
    "vecs": ((PAIRS, TILE, 4 * TILE), jnp.bfloat16),
    "weighted": ((PAIRS, TILE, 4 * TILE), jnp.bfloat16),
    "window0": ((3 * PAIRS, TILE, TILE), jnp.bfloat16),
    "window1": ((3 * PAIRS, TILE, TILE), jnp.bfloat16),
    "window2": ((3 * PAIRS, TILE, TILE), jnp.bfloat16),
    "inverse": ((PAIRS, TILE, TILE), jnp.float32),
    "integ": ((PAIRS, TILE, TILE), jnp.float32),
    "factor": ((PAIRS, TILE, TILE), jnp.float32),
    "own_part": ((CHUNK, TILE, TILE), jnp.float32),
    "share_out": ((AUXES - 1, CHUNK, TILE, TILE), jnp.bfloat16),
    "share_in": ((AUXES - 1, CHUNK, TILE, TILE), jnp.bfloat16),
    "high": ((PAIRS, TILE, TILE), jnp.bfloat16),
    "low": ((PAIRS, TILE, TILE), jnp.bfloat16),
    "local_sem": (2,),
    "x_send": (3, AUXES - 1),
    "x_recv": (3, AUXES - 1),
    "halo_send": (ITERS, 2),
    "halo_recv": (ITERS, 2),
}


def exchange_scratch(extra):
    return {
        "coef": ((PAIRS, DOM * TILE, TILE), jnp.bfloat16),
        "outgoing": ((DIRECT * OWNERS, TILE, TILE), jnp.bfloat16),
        "landing": ((DIRECT * OWNERS + extra * PLANES, TILE, TILE), jnp.bfloat16),
        "relay_out": ((OWNERS, TILE, TILE), jnp.bfloat16),
        "relay_in": ((OWNERS, TILE, TILE), jnp.bfloat16),
        "extra_out": ((extra * PLANES, TILE, TILE), jnp.bfloat16),
        "block_sem": (6,),
    }


SEND = 0
RELAY = SEND + CAP * PLANES
LAND = RELAY + max(EXTRAS) * PLANES
ROWS = LAND + REQ
SUM, HIGH, LOW = range(3)


def kernel(extra, *refs):
    exchanging = extra > 0
    names = ["table", "count", "occ", "source", "coef_hbm", "energy", "near", "coupling", "inter_hbm", "amp", "pair_energy"]
    names += list(SCRATCH) + (list(exchange_scratch(extra)) if exchanging else [])
    if not exchanging:
        names.remove("coef_hbm")
    r = types.SimpleNamespace(**dict(zip(names, refs, strict=True)))
    me, ax = lax.axis_index("pair"), lax.axis_index("aux")
    plane, col = me // COLS, me % COLS
    y, core = col // 2, col % 2
    left, right = lax.rem(me + OWNERS - 1, OWNERS), lax.rem(me + 1, OWNERS)
    own = pl.multiple_of(ax * CHUNK, CHUNK)
    peers = [lax.rem(ax + k, AUXES) for k in range(AUXES)]
    windows = (r.window0, r.window1, r.window2)

    barrier = pltpu.get_barrier_semaphore()
    for k in range(1, AUXES):
        pl.semaphore_signal(barrier, inc=1, device_id=(me, peers[k]), device_id_type=MESH)
    if exchanging:

        def greet(k, carry):
            pl.semaphore_signal(barrier, inc=1, device_id=(lax.rem(me + k, OWNERS), ax), device_id_type=MESH)
            return carry

        lax.fori_loop(1, OWNERS, greet, 0)
        greeted = AUXES - 1 + OWNERS - 1
    else:
        for side in (left, right):
            pl.semaphore_signal(barrier, inc=1, device_id=(side, ax), device_id_type=MESH)
        greeted = AUXES - 1 + 2

    inter_copy = pltpu.make_async_copy(r.inter_hbm, r.inter, r.local_sem.at[0])
    if exchanging:
        coef_copy = pltpu.make_async_copy(r.coef_hbm, r.coef, r.local_sem.at[1])

    rows = lax.broadcasted_iota(jnp.int32, (TILE, TILE), 0)
    columns = lax.broadcasted_iota(jnp.int32, (TILE, TILE), 1)

    def masked(q, values):
        return jnp.where((rows < r.count[q]) & (columns < r.count[q]), values, 0.0)

    def prepare():
        def denominators(q, carry):
            across = jnp.broadcast_to(r.energy[pl.ds(q, 1), :], (TILE, TILE))
            r.inverse[q] = masked(q, 1.0 / (across + across.T + r.occ[q]))
            return carry

        lax.fori_loop(0, PAIRS, denominators, 0)
        inter_copy.wait()

        def narrow(q, carry):
            for n in range(4):
                v = r.inter[q, n]
                cut = slice(n * TILE, (n + 1) * TILE)
                r.vecs[q, :, cut] = v.astype(jnp.bfloat16)
                r.weighted[q, :, cut] = (v * r.coupling[n, q]).astype(jnp.bfloat16)
            return carry

        lax.fori_loop(0, PAIRS, narrow, 0)

    if exchanging:
        blocks, outgoing, landing = r.source, r.outgoing, r.landing

        def fill(k, carry):
            dst = lax.rem(me + k, OWNERS)
            for s in range(DIRECT):
                outgoing[DIRECT * k + s] = blocks[r.table[SEND + s * PLANES + dst // COLS, dst % COLS]]
            return carry

        def fill_relay(i, carry):
            k, b = i // PLANES, i % PLANES
            r.relay_out[i] = blocks[r.table[SEND + DIRECT * PLANES + b, lax.rem(col + k, COLS)]]
            return carry

        lax.fori_loop(0, OWNERS, fill, 0)
        lax.fori_loop(0, OWNERS, fill_relay, 0)
        for s in range(DIRECT):
            landing[s] = outgoing[s]
        for b in range(PLANES):
            r.relay_in[b] = r.relay_out[b]

        def whole(source, target, first, count, sem):
            return pltpu.make_async_remote_copy(
                src_ref=source.at[pl.ds(first, count)], dst_ref=target.at[pl.ds(first, count)],
                send_sem=r.block_sem.at[sem], recv_sem=r.block_sem.at[sem + 1],
                device_id=(right, ax), device_id_type=MESH,
            )

        def direct(dst):
            to, back = lax.rem(dst - me + OWNERS, OWNERS), lax.rem(me - dst + OWNERS, OWNERS)
            return pltpu.make_async_remote_copy(
                src_ref=outgoing.at[pl.ds(DIRECT * to, DIRECT)],
                dst_ref=landing.at[pl.ds(DIRECT * back, DIRECT)],
                send_sem=r.block_sem.at[0], recv_sem=r.block_sem.at[1],
                device_id=(dst, ax), device_id_type=MESH,
            )

        def to_relay(k):
            return pltpu.make_async_remote_copy(
                src_ref=r.relay_out.at[pl.ds(PLANES * k, PLANES)],
                dst_ref=r.relay_in.at[pl.ds(PLANES * (COLS - k), PLANES)],
                send_sem=r.block_sem.at[2], recv_sem=r.block_sem.at[3],
                device_id=(plane * COLS + lax.rem(col + k, COLS), ax), device_id_type=MESH,
            )

        def from_relay(k):
            return pltpu.make_async_remote_copy(
                src_ref=r.extra_out.at[pl.ds(extra * k, extra)],
                dst_ref=landing.at[pl.ds(DIRECT * OWNERS + extra * (PLANES - k), extra)],
                send_sem=r.block_sem.at[4], recv_sem=r.block_sem.at[5],
                device_id=(lax.rem(plane + k, PLANES) * COLS + col, ax), device_id_type=MESH,
            )

        pl.semaphore_wait(barrier, greeted)
        for k in range(1, COLS):
            to_relay(k).start()
        for dz, dy, dc in STEPS:
            direct(
                lax.rem(plane + dz, PLANES) * COLS + lax.rem(y + dy, 4) * 2 + lax.rem(core + dc, 2)
            ).start()
        inter_copy.start()
        coef_copy.start()
        prepare()

        relayed = whole(r.relay_out, r.relay_in, PLANES, PLANES * (COLS - 1), 2)
        relayed.wait_recv()
        for k in (4, 3, 5, 2, 6, 1, 7, 0):
            b = lax.rem(plane + k, PLANES)
            for e in range(extra):
                block = r.relay_in[r.table[RELAY + e * PLANES + b, col]]
                if k == 0:
                    landing[DIRECT * OWNERS + e] = block
                else:
                    r.extra_out[extra * k + e] = block
            if k != 0:
                from_relay(k).start()

        coef_copy.wait()
        relayed.wait_send()
        sent = whole(outgoing, landing, DIRECT, DIRECT * (OWNERS - 1), 0)
        sent.wait_send()
        sent.wait_recv()
        extras = pltpu.make_async_remote_copy(
            src_ref=r.extra_out.at[pl.ds(extra, extra * (PLANES - 1))],
            dst_ref=landing.at[pl.ds(DIRECT * OWNERS + extra, extra * (PLANES - 1))],
            send_sem=r.block_sem.at[4], recv_sem=r.block_sem.at[5],
            device_id=(right, ax), device_id_type=MESH,
        )
        extras.wait_send()
        extras.wait_recv()

        def part(q):
            rows_of = [
                jnp.concatenate(
                    [landing[r.table[LAND + m * DOM + t, col * PAIRS + q]] for t in range(DOM)], axis=1
                )
                for m in range(2)
            ]
            projected = jnp.dot(
                jnp.concatenate(rows_of, axis=0), r.coef[q], preferred_element_type=jnp.float32
            ).astype(jnp.bfloat16)
            return lax.dot_general(
                projected[:TILE], projected[TILE:], (((0,), (0,)), ((), ())),
                preferred_element_type=jnp.float32,
            )

    else:
        inter_copy.start()
        prepare()
        pl.semaphore_wait(barrier, greeted)

        def part(q):
            return r.source[q]

    def share(k):
        return pltpu.make_async_remote_copy(
            src_ref=r.share_out.at[k - 1], dst_ref=r.share_in.at[AUXES - 1 - k],
            send_sem=r.x_send.at[SUM, k - 1], recv_sem=r.x_recv.at[SUM, AUXES - 1 - k],
            device_id=(me, peers[k]), device_id_type=MESH,
        )

    def spread(kind, k):
        values = r.high if kind == HIGH else r.low
        return pltpu.make_async_remote_copy(
            src_ref=values.at[pl.ds(own, CHUNK)], dst_ref=values.at[pl.ds(own, CHUNK)],
            send_sem=r.x_send.at[kind, k - 1], recv_sem=r.x_recv.at[kind, AUXES - 1 - k],
            device_id=(me, peers[k]), device_id_type=MESH,
        )

    def wait_shares():
        for k in range(1, AUXES):
            pltpu.make_async_remote_copy(
                src_ref=r.share_in.at[k - 1], dst_ref=r.share_in.at[k - 1],
                send_sem=r.x_send.at[SUM, k - 1], recv_sem=r.x_recv.at[SUM, k - 1],
                device_id=(me, peers[k]), device_id_type=MESH,
            ).wait_recv()

    def wait_spread(kind, k):
        values = r.high if kind == HIGH else r.low
        theirs = values.at[pl.ds(peers[k] * CHUNK, CHUNK)]
        pltpu.make_async_remote_copy(
            src_ref=theirs, dst_ref=theirs,
            send_sem=r.x_send.at[kind, k - 1], recv_sem=r.x_recv.at[kind, k - 1],
            device_id=(me, peers[k]), device_id_type=MESH,
        ).wait_recv()

    def halo(sweep, first, size, side):
        target = first + 2 * PAIRS if side == 0 else first
        return pltpu.make_async_remote_copy(
            src_ref=windows[sweep].at[pl.ds(PAIRS + first, size)],
            dst_ref=windows[sweep].at[pl.ds(target, size)],
            send_sem=r.halo_send.at[sweep, side], recv_sem=r.halo_recv.at[sweep, side],
            device_id=(left if side == 0 else right, ax), device_id_type=MESH,
        )

    def wait_halo(sweep):
        for side in range(2):
            done = pltpu.make_async_remote_copy(
                src_ref=windows[sweep].at[pl.ds(PAIRS, PAIRS)],
                dst_ref=windows[sweep].at[pl.ds(2 * PAIRS if side == 0 else 0, PAIRS)],
                send_sem=r.halo_send.at[sweep, side], recv_sem=r.halo_recv.at[sweep, side],
                device_id=(left if side == 0 else right, ax), device_id_type=MESH,
            )
            done.wait_send()
            done.wait_recv()

    for k in (2, 1, 3):
        for i in range(CHUNK):
            r.share_out[k - 1, i] = part(peers[k] * CHUNK + i).astype(jnp.bfloat16)
        share(k).start()
    for i in range(CHUNK):
        r.own_part[i] = part(own + i)
    wait_shares()

    def add(i, carry):
        values = r.own_part[i]
        for k in range(AUXES - 1):
            values = values + r.share_in[k, i].astype(jnp.float32)
        values = masked(own + i, values)
        top = values.astype(jnp.bfloat16)
        r.high[own + i] = top
        r.low[own + i] = (values - top.astype(jnp.float32)).astype(jnp.bfloat16)
        return carry

    lax.fori_loop(0, CHUNK, add, 0)
    for k in (2, 1, 3):
        spread(HIGH, k).start()

    def first_amplitudes(start):
        def body(i, carry):
            q = start + i
            windows[0][PAIRS + q] = (-r.high[q].astype(jnp.float32) * r.inverse[q]).astype(jnp.bfloat16)
            return carry

        lax.fori_loop(0, CHUNK, body, 0)
        for side in range(2):
            halo(0, start, CHUNK, side).start()

    first_amplitudes(own)
    for k in (1, 3, 2):
        wait_spread(HIGH, k)
        first_amplitudes(pl.multiple_of(peers[k] * CHUNK, CHUNK))
    for k in (2, 1, 3):
        spread(LOW, k).start()

    def both_halves(q, carry):
        integrals = r.high[q].astype(jnp.float32) + r.low[q].astype(jnp.float32)
        r.integ[q] = integrals
        r.factor[q] = 2.0 * integrals - integrals.T
        return carry

    for sweep in range(ITERS):
        if sweep == ITERS - 1:
            for k in (1, 3, 2):
                wait_spread(LOW, k)
            lax.fori_loop(0, PAIRS, both_halves, 0)
        wait_halo(sweep)

        def update(q, sweep=sweep):
            firsts = [
                jnp.dot(
                    r.weighted[q, :, n * TILE : (n + 1) * TILE],
                    windows[sweep][jnp.clip(r.near[n, q] - (me - 1) * PAIRS, 0, 3 * PAIRS - 1)],
                    preferred_element_type=jnp.float32,
                ).astype(jnp.bfloat16)
                for n in range(4)
            ]
            coupled = lax.dot_general(
                jnp.concatenate(firsts, axis=1), r.vecs[q], (((1,), (1,)), ((), ())),
                preferred_element_type=jnp.float32,
            )
            integrals = r.high[q].astype(jnp.float32) if sweep < ITERS - 1 else r.integ[q]
            current = (coupled - integrals) * r.inverse[q]
            if sweep < ITERS - 1:
                windows[sweep + 1][PAIRS + q] = current.astype(jnp.bfloat16)
            else:
                r.amp[q] = current
                r.pair_energy[q] = jnp.sum(r.factor[q] * current)

        def some(j, carry, sweep=sweep):
            for i in range(CHUNK):
                update(j * CHUNK + i)
            if sweep < ITERS - 1:
                for side in range(2):
                    halo(sweep + 1, pl.multiple_of(j * CHUNK, CHUNK), CHUNK, side).start()
            return carry

        lax.fori_loop(0, PAIRS // CHUNK, some, 0)

    for k in range(1, AUXES):
        share(k).wait_send()
        for kind in (HIGH, LOW):
            spread(kind, k).wait_send()


def run_kernel(extra, table, count, occ, source, coef, energy, near, coupling, inter):
    exchanging = extra > 0
    smem, vmem = pl.BlockSpec(memory_space=pltpu.SMEM), pl.BlockSpec(memory_space=pltpu.VMEM)
    hbm = pl.BlockSpec(memory_space=pl.ANY)
    scratch = dict(SCRATCH, **(exchange_scratch(extra) if exchanging else {}))
    return pl.pallas_call(
        functools.partial(kernel, extra),
        out_shape=(
            jax.ShapeDtypeStruct((PAIRS, TILE, TILE), jnp.float32),
            jax.ShapeDtypeStruct((PAIRS,), jnp.float32),
        ),
        in_specs=[smem, smem, smem, vmem] + [hbm] * exchanging + [vmem, smem, smem, hbm],
        out_specs=(vmem, smem),
        scratch_shapes=[
            pltpu.SemaphoreType.DMA(v) if isinstance(v[0], int) else pltpu.VMEM(*v) for v in scratch.values()
        ],
        compiler_params=pltpu.CompilerParams(
            collective_id=extra, has_side_effects=True, vmem_limit_bytes=VMEM_LIMIT
        ),
    )(*([table, count, occ, source] + [coef] * exchanging + [energy, near, coupling, inter]))


def padded_exchange(blocks, coef, source_dev, block_pos, me):
    source = source_dev.reshape(OWNERS, TOTAL)
    position = block_pos.reshape(OWNERS, TOTAL)
    wanted = source == me
    ranking = jnp.cumsum(wanted.astype(jnp.int32), axis=1) - 1
    slots = jnp.arange(CAP, dtype=jnp.int32)
    chosen = wanted[:, None, :] & (ranking[:, None, :] == slots[None, :, None])
    send_pos = jnp.sum(jnp.where(chosen, position[:, None, :], 0), axis=2)
    incoming = lax.all_to_all(
        blocks[send_pos], "pair", split_axis=0, concat_axis=0, tiled=True
    )
    own_source = lax.dynamic_index_in_dim(source, me, 0, keepdims=False)
    order = jnp.arange(TOTAL, dtype=jnp.int32)
    earlier = (own_source[None, :] == own_source[:, None]) & (order[None, :] < order[:, None])
    own_rank = jnp.sum(earlier.astype(jnp.int32), axis=1)
    arrived = incoming.reshape((OWNERS * CAP,) + blocks.shape[1:])[own_source * CAP + own_rank]
    arrived = arrived.reshape((PAIRS, 2, DOM) + blocks.shape[1:])
    coefs = coef.reshape(PAIRS, DOM, TILE, TILE)
    projected = jnp.einsum(
        "qmtxp,qtpn->qmxn", arrived, coefs, preferred_element_type=jnp.float32
    ).astype(jnp.bfloat16)
    return jnp.einsum(
        "qxa,qxb->qab", projected[:, 0], projected[:, 1], preferred_element_type=jnp.float32
    )


def route_kernel(source, position, table, most, by_tile, taken):
    me = lax.axis_index("pair")
    plane, col = me // COLS, me % COLS
    lanes = PAIRS * COLS
    for c in range(REQ):
        for j in range(PLANES):
            cut = slice(j * lanes, (j + 1) * lanes)
            by_tile[0, c, j : j + 1, :] = source[c : c + 1, cut]
            by_tile[1, c, j : j + 1, :] = position[c : c + 1, cut]
    row = lax.broadcasted_iota(jnp.int32, (lanes, lanes), 0)
    lane = lax.broadcasted_iota(jnp.int32, (lanes, lanes), 1)
    earlier = ((row // PAIRS == lane // PAIRS) & (row < lane)).astype(jnp.float32)
    device = (row // PAIRS == lane).astype(jnp.float32)

    wanted = jnp.zeros((PLANES, lanes), jnp.float32)
    where = jnp.zeros((PLANES, lanes), jnp.float32)
    for c in range(REQ):
        hit = by_tile[0, c] == me
        wanted = wanted + jnp.where(hit, 1.0, 0.0)
        where = where + jnp.where(hit, by_tile[1, c].astype(jnp.float32), 0.0)
    rank = jnp.dot(wanted, earlier, preferred_element_type=jnp.float32)
    for s in range(CAP):
        chosen = jnp.where(rank == s, where, 0.0)
        table[SEND + s * PLANES : SEND + (s + 1) * PLANES, :] = jnp.dot(
            chosen, device, preferred_element_type=jnp.float32
        ).astype(jnp.int32)

    for s in range(OWNERS):
        count = jnp.zeros((PLANES, lanes), jnp.float32)
        for c in range(REQ):
            count = count + jnp.where(by_tile[0, c] == s, 1.0, 0.0)
        taken[s] = count
    counts = jnp.dot(
        taken[...].reshape(OWNERS * PLANES, lanes), device, preferred_element_type=jnp.float32
    )
    taken[...] = jnp.where(counts > DIRECT, 1.0, 0.0).reshape(OWNERS, PLANES, lanes)
    worst = jnp.zeros((PLANES, lanes), jnp.float32)
    for a in range(PLANES):
        total = taken[a * COLS]
        for k in range(1, COLS):
            total = total + taken[a * COLS + k]
        worst = jnp.maximum(worst, total)
    worst = jnp.max(worst).astype(jnp.int32)
    most[0] = worst

    planes = lax.broadcasted_iota(jnp.int32, (PLANES, lanes), 0)
    before = jnp.zeros((PLANES, lanes), jnp.float32)
    picked = [jnp.zeros((PLANES, lanes), jnp.int32) for _ in range(max(EXTRAS))]
    for k in range(COLS):
        third = taken[plane * COLS + k]
        back = lax.rem(k - col + COLS, COLS)
        for e in range(max(EXTRAS)):
            picked[e] = picked[e] + jnp.where((third > 0.0) & (before == e), back, 0)
        before = before + third
    for e in range(max(EXTRAS)):
        first = RELAY + e * PLANES
        table[first : first + PLANES, :] = picked[e] * PLANES + planes

    mine = source[:, pl.ds(pl.multiple_of(plane * lanes, lanes), lanes)]
    place = lax.broadcasted_iota(jnp.int32, (REQ, lanes), 1) % PAIRS

    def others(values, shift):
        if shift:
            inside = (place >= shift) & (place < PAIRS + shift)
            values = jnp.where(inside, pltpu.roll(values, shift % lanes, 1), -1)
        return [values] + [pltpu.roll(values, k, 0) for k in range(1, REQ)]

    own_rank = jnp.zeros((REQ, lanes), jnp.int32)
    for shift in range(1, PAIRS):
        for other in others(mine, shift):
            own_rank = own_rank + jnp.where(other == mine, 1, 0)
    thirds = jnp.where(own_rank >= DIRECT, mine, -1)
    first_of_plane = mine - mine % COLS
    extra_rank = jnp.zeros((REQ, lanes), jnp.int32)
    for shift in range(1 - PAIRS, PAIRS):
        for other in others(thirds, shift):
            extra_rank = extra_rank + jnp.where((other >= first_of_plane) & (other < mine), 1, 0)
    room = jnp.clip(worst, EXTRAS[0], EXTRAS[1])
    extra_row = (
        DIRECT * OWNERS
        + ((mine // COLS - plane + PLANES) % PLANES) * room
        + jnp.minimum(extra_rank, room - 1)
    )
    direct_row = ((mine - me + OWNERS) % OWNERS) * DIRECT + own_rank
    table[LAND : LAND + REQ, :] = jnp.where(own_rank >= DIRECT, extra_row, direct_row)


def route(source_dev, block_pos):
    vmem = pl.BlockSpec(memory_space=pltpu.VMEM)
    lanes = PAIRS * COLS
    return pl.pallas_call(
        route_kernel,
        out_shape=(
            jax.ShapeDtypeStruct((ROWS, lanes), jnp.int32),
            jax.ShapeDtypeStruct((1,), jnp.int32),
        ),
        in_specs=[vmem, vmem],
        out_specs=(vmem, pl.BlockSpec(memory_space=pltpu.SMEM)),
        scratch_shapes=[
            pltpu.VMEM((2, REQ, PLANES, lanes), jnp.int32),
            pltpu.VMEM((OWNERS, PLANES, lanes), jnp.float32),
        ],
    )(source_dev.T, block_pos.T)


def shards(
    blocks, pno_coef, source_dev, block_pos, pno_energy, occ_energy, pno_count, neighbour, coupling, intersection,
):
    me = lax.axis_index("pair")
    table, most = route(source_dev, block_pos)

    def finish(extra, source):
        return run_kernel(
            extra, table, pno_count, occ_energy, source, pno_coef, pno_energy, neighbour.T, coupling.T, intersection
        )

    return lax.switch(
        jnp.clip(most[0], 1, 3) - 1,
        [
            lambda: finish(1, blocks),
            lambda: finish(2, blocks),
            lambda: finish(0, padded_exchange(blocks, pno_coef, source_dev, block_pos, me)),
        ],
    )


def solution(mesh):
    return jax.shard_map(
        shards,
        mesh=mesh,
        in_specs=(
            P("pair", "aux", None),
            P("pair", None, None),
            P(),
            P(),
            P("pair", None),
            P("pair"),
            P("pair"),
            P("pair", None),
            P("pair", None),
            P("pair", None, None, None),
        ),
        out_specs=(P("pair", None, None), P("pair")),
        check_vma=False,
    )
```

```python
import functools
import types

import jax
import jax.numpy as jnp
from jax import lax
from jax.experimental import pallas as pl
from jax.experimental.pallas import tpu as pltpu
from jax.sharding import PartitionSpec as P

ITERS = 3
MESH = pl.DeviceIdType.MESH

PLANES = 8
COLS = 8
OWNERS = PLANES * COLS
AUXES = 4
PAIRS = 16
REQ = 8
DOM = 4
BLOCKS = 64
TOTAL = PAIRS * REQ
TILE = 128
CAP = 3
DIRECT = 2
EXTRAS = (1, 2)

VMEM_LIMIT = 56 * 2**20
CHUNK = PAIRS // AUXES


def distance(step):
    dz, dy, _ = step
    return min(dz, PLANES - dz) + min(dy, 4 - dy)


STEPS = sorted(
    [(dz, dy, dc) for dz in range(PLANES) for dy in range(4) for dc in range(2) if (dz, dy, dc) != (0, 0, 0)],
    key=lambda s: -distance(s),
)


SCRATCH = {
    "inter": ((PAIRS, 4, TILE, TILE), jnp.float32),
    "vecs": ((PAIRS, TILE, 4 * TILE), jnp.bfloat16),
    "weighted": ((PAIRS, TILE, 4 * TILE), jnp.bfloat16),
    "window0": ((3 * PAIRS, TILE, TILE), jnp.bfloat16),
    "window1": ((3 * PAIRS, TILE, TILE), jnp.bfloat16),
    "window2": ((3 * PAIRS, TILE, TILE), jnp.bfloat16),
    "inverse": ((PAIRS, TILE, TILE), jnp.float32),
    "integ": ((PAIRS, TILE, TILE), jnp.float32),
    "factor": ((PAIRS, TILE, TILE), jnp.float32),
    "own_part": ((CHUNK, TILE, TILE), jnp.float32),
    "share_out": ((AUXES - 1, CHUNK, TILE, TILE), jnp.bfloat16),
    "share_in": ((AUXES - 1, CHUNK, TILE, TILE), jnp.bfloat16),
    "high": ((PAIRS, TILE, TILE), jnp.bfloat16),
    "low": ((PAIRS, TILE, TILE), jnp.bfloat16),
    "local_sem": (2,),
    "x_send": (3, AUXES - 1),
    "x_recv": (3, AUXES - 1),
    "halo_send": (ITERS, 2),
    "halo_recv": (ITERS, 2),
}


def exchange_scratch(extra):
    return {
        "coef": ((PAIRS, DOM * TILE, TILE), jnp.bfloat16),
        "outgoing": ((DIRECT * OWNERS, TILE, TILE), jnp.bfloat16),
        "landing": ((DIRECT * OWNERS + extra * PLANES, TILE, TILE), jnp.bfloat16),
        "relay_out": ((OWNERS, TILE, TILE), jnp.bfloat16),
        "relay_in": ((OWNERS, TILE, TILE), jnp.bfloat16),
        "extra_out": ((extra * PLANES, TILE, TILE), jnp.bfloat16),
        "block_sem": (6,),
    }


SEND = 0
RELAY = SEND + CAP * PLANES
LAND = RELAY + max(EXTRAS) * PLANES
ROWS = LAND + REQ
SUM, HIGH, LOW = range(3)


def kernel(extra, *refs):
    exchanging = extra > 0
    names = ["table", "count", "occ", "source", "coef_hbm", "energy", "near", "coupling", "inter_hbm", "amp", "pair_energy"]
    names += list(SCRATCH) + (list(exchange_scratch(extra)) if exchanging else [])
    if not exchanging:
        names.remove("coef_hbm")
    r = types.SimpleNamespace(**dict(zip(names, refs, strict=True)))
    me, ax = lax.axis_index("pair"), lax.axis_index("aux")
    plane, col = me // COLS, me % COLS
    y, core = col // 2, col % 2
    left, right = lax.rem(me + OWNERS - 1, OWNERS), lax.rem(me + 1, OWNERS)
    own = pl.multiple_of(ax * CHUNK, CHUNK)
    peers = [lax.rem(ax + k, AUXES) for k in range(AUXES)]
    windows = (r.window0, r.window1, r.window2)

    barrier = pltpu.get_barrier_semaphore()
    for k in range(1, AUXES):
        pl.semaphore_signal(barrier, inc=1, device_id=(me, peers[k]), device_id_type=MESH)
    if exchanging:

        def greet(k, carry):
            pl.semaphore_signal(barrier, inc=1, device_id=(lax.rem(me + k, OWNERS), ax), device_id_type=MESH)
            return carry

        lax.fori_loop(1, OWNERS, greet, 0)
        greeted = AUXES - 1 + OWNERS - 1
    else:
        for side in (left, right):
            pl.semaphore_signal(barrier, inc=1, device_id=(side, ax), device_id_type=MESH)
        greeted = AUXES - 1 + 2

    inter_copy = pltpu.make_async_copy(r.inter_hbm, r.inter, r.local_sem.at[0])
    if exchanging:
        coef_copy = pltpu.make_async_copy(r.coef_hbm, r.coef, r.local_sem.at[1])

    rows = lax.broadcasted_iota(jnp.int32, (TILE, TILE), 0)
    columns = lax.broadcasted_iota(jnp.int32, (TILE, TILE), 1)

    def masked(q, values):
        return jnp.where((rows < r.count[q]) & (columns < r.count[q]), values, 0.0)

    def prepare():
        def denominators(q, carry):
            across = jnp.broadcast_to(r.energy[pl.ds(q, 1), :], (TILE, TILE))
            r.inverse[q] = masked(q, 1.0 / (across + across.T + r.occ[q]))
            return carry

        lax.fori_loop(0, PAIRS, denominators, 0)
        inter_copy.wait()

        def narrow(q, carry):
            for n in range(4):
                v = r.inter[q, n]
                cut = slice(n * TILE, (n + 1) * TILE)
                r.vecs[q, :, cut] = v.astype(jnp.bfloat16)
                r.weighted[q, :, cut] = (v * r.coupling[n, q]).astype(jnp.bfloat16)
            return carry

        lax.fori_loop(0, PAIRS, narrow, 0)

    if exchanging:
        blocks, outgoing, landing = r.source, r.outgoing, r.landing

        def fill(k, carry):
            dst = lax.rem(me + k, OWNERS)
            for s in range(DIRECT):
                outgoing[DIRECT * k + s] = blocks[r.table[SEND + s * PLANES + dst // COLS, dst % COLS]]
            return carry

        def fill_relay(i, carry):
            k, b = i // PLANES, i % PLANES
            r.relay_out[i] = blocks[r.table[SEND + DIRECT * PLANES + b, lax.rem(col + k, COLS)]]
            return carry

        lax.fori_loop(0, OWNERS, fill, 0)
        lax.fori_loop(0, OWNERS, fill_relay, 0)
        for s in range(DIRECT):
            landing[s] = outgoing[s]
        for b in range(PLANES):
            r.relay_in[b] = r.relay_out[b]

        def whole(source, target, first, count, sem):
            return pltpu.make_async_remote_copy(
                src_ref=source.at[pl.ds(first, count)], dst_ref=target.at[pl.ds(first, count)],
                send_sem=r.block_sem.at[sem], recv_sem=r.block_sem.at[sem + 1],
                device_id=(right, ax), device_id_type=MESH,
            )

        def direct(dst):
            to, back = lax.rem(dst - me + OWNERS, OWNERS), lax.rem(me - dst + OWNERS, OWNERS)
            return pltpu.make_async_remote_copy(
                src_ref=outgoing.at[pl.ds(DIRECT * to, DIRECT)],
                dst_ref=landing.at[pl.ds(DIRECT * back, DIRECT)],
                send_sem=r.block_sem.at[0], recv_sem=r.block_sem.at[1],
                device_id=(dst, ax), device_id_type=MESH,
            )

        def to_relay(k):
            return pltpu.make_async_remote_copy(
                src_ref=r.relay_out.at[pl.ds(PLANES * k, PLANES)],
                dst_ref=r.relay_in.at[pl.ds(PLANES * (COLS - k), PLANES)],
                send_sem=r.block_sem.at[2], recv_sem=r.block_sem.at[3],
                device_id=(plane * COLS + lax.rem(col + k, COLS), ax), device_id_type=MESH,
            )

        def from_relay(k):
            return pltpu.make_async_remote_copy(
                src_ref=r.extra_out.at[pl.ds(extra * k, extra)],
                dst_ref=landing.at[pl.ds(DIRECT * OWNERS + extra * (PLANES - k), extra)],
                send_sem=r.block_sem.at[4], recv_sem=r.block_sem.at[5],
                device_id=(lax.rem(plane + k, PLANES) * COLS + col, ax), device_id_type=MESH,
            )

        pl.semaphore_wait(barrier, greeted)
        for k in range(1, COLS):
            to_relay(k).start()
        for dz, dy, dc in STEPS:
            direct(
                lax.rem(plane + dz, PLANES) * COLS + lax.rem(y + dy, 4) * 2 + lax.rem(core + dc, 2)
            ).start()
        inter_copy.start()
        coef_copy.start()
        prepare()

        relayed = whole(r.relay_out, r.relay_in, PLANES, PLANES * (COLS - 1), 2)
        relayed.wait_recv()
        for k in (4, 3, 5, 2, 6, 1, 7, 0):
            b = lax.rem(plane + k, PLANES)
            for e in range(extra):
                block = r.relay_in[r.table[RELAY + e * PLANES + b, col]]
                if k == 0:
                    landing[DIRECT * OWNERS + e] = block
                else:
                    r.extra_out[extra * k + e] = block
            if k != 0:
                from_relay(k).start()

        coef_copy.wait()
        relayed.wait_send()
        sent = whole(outgoing, landing, DIRECT, DIRECT * (OWNERS - 1), 0)
        sent.wait_send()
        sent.wait_recv()
        extras = pltpu.make_async_remote_copy(
            src_ref=r.extra_out.at[pl.ds(extra, extra * (PLANES - 1))],
            dst_ref=landing.at[pl.ds(DIRECT * OWNERS + extra, extra * (PLANES - 1))],
            send_sem=r.block_sem.at[4], recv_sem=r.block_sem.at[5],
            device_id=(right, ax), device_id_type=MESH,
        )
        extras.wait_send()
        extras.wait_recv()

        def part(q):
            rows_of = [
                jnp.concatenate(
                    [landing[r.table[LAND + m * DOM + t, col * PAIRS + q]] for t in range(DOM)], axis=1
                )
                for m in range(2)
            ]
            projected = jnp.dot(
                jnp.concatenate(rows_of, axis=0), r.coef[q], preferred_element_type=jnp.float32
            ).astype(jnp.bfloat16)
            return lax.dot_general(
                projected[:TILE], projected[TILE:], (((0,), (0,)), ((), ())),
                preferred_element_type=jnp.float32,
            )

    else:
        inter_copy.start()
        prepare()
        pl.semaphore_wait(barrier, greeted)

        def part(q):
            return r.source[q]

    def share(k):
        return pltpu.make_async_remote_copy(
            src_ref=r.share_out.at[k - 1], dst_ref=r.share_in.at[AUXES - 1 - k],
            send_sem=r.x_send.at[SUM, k - 1], recv_sem=r.x_recv.at[SUM, AUXES - 1 - k],
            device_id=(me, peers[k]), device_id_type=MESH,
        )

    def spread(kind, k):
        values = r.high if kind == HIGH else r.low
        return pltpu.make_async_remote_copy(
            src_ref=values.at[pl.ds(own, CHUNK)], dst_ref=values.at[pl.ds(own, CHUNK)],
            send_sem=r.x_send.at[kind, k - 1], recv_sem=r.x_recv.at[kind, AUXES - 1 - k],
            device_id=(me, peers[k]), device_id_type=MESH,
        )

    def wait_shares():
        for k in range(1, AUXES):
            pltpu.make_async_remote_copy(
                src_ref=r.share_in.at[k - 1], dst_ref=r.share_in.at[k - 1],
                send_sem=r.x_send.at[SUM, k - 1], recv_sem=r.x_recv.at[SUM, k - 1],
                device_id=(me, peers[k]), device_id_type=MESH,
            ).wait_recv()

    def wait_spread(kind, k):
        values = r.high if kind == HIGH else r.low
        theirs = values.at[pl.ds(peers[k] * CHUNK, CHUNK)]
        pltpu.make_async_remote_copy(
            src_ref=theirs, dst_ref=theirs,
            send_sem=r.x_send.at[kind, k - 1], recv_sem=r.x_recv.at[kind, k - 1],
            device_id=(me, peers[k]), device_id_type=MESH,
        ).wait_recv()

    def halo(sweep, first, size, side):
        target = first + 2 * PAIRS if side == 0 else first
        return pltpu.make_async_remote_copy(
            src_ref=windows[sweep].at[pl.ds(PAIRS + first, size)],
            dst_ref=windows[sweep].at[pl.ds(target, size)],
            send_sem=r.halo_send.at[sweep, side], recv_sem=r.halo_recv.at[sweep, side],
            device_id=(left if side == 0 else right, ax), device_id_type=MESH,
        )

    def wait_halo(sweep):
        for side in range(2):
            done = pltpu.make_async_remote_copy(
                src_ref=windows[sweep].at[pl.ds(PAIRS, PAIRS)],
                dst_ref=windows[sweep].at[pl.ds(2 * PAIRS if side == 0 else 0, PAIRS)],
                send_sem=r.halo_send.at[sweep, side], recv_sem=r.halo_recv.at[sweep, side],
                device_id=(left if side == 0 else right, ax), device_id_type=MESH,
            )
            done.wait_send()
            done.wait_recv()

    for k in (1, 3, 2):
        for i in range(CHUNK):
            r.share_out[k - 1, i] = part(peers[k] * CHUNK + i).astype(jnp.bfloat16)
        share(k).start()
    for i in range(CHUNK):
        r.own_part[i] = part(own + i)
    wait_shares()

    def add(i, carry):
        values = r.own_part[i]
        for k in range(AUXES - 1):
            values = values + r.share_in[k, i].astype(jnp.float32)
        values = masked(own + i, values)
        top = values.astype(jnp.bfloat16)
        r.high[own + i] = top
        r.low[own + i] = (values - top.astype(jnp.float32)).astype(jnp.bfloat16)
        return carry

    lax.fori_loop(0, CHUNK, add, 0, unroll=True)
    for k in (1, 3, 2):
        spread(HIGH, k).start()

    def first_amplitudes(start):
        def body(i, carry):
            q = start + i
            windows[0][PAIRS + q] = (-r.high[q].astype(jnp.float32) * r.inverse[q]).astype(jnp.bfloat16)
            return carry

        lax.fori_loop(0, CHUNK, body, 0, unroll=True)
        for side in range(2):
            halo(0, start, CHUNK, side).start()

    first_amplitudes(own)
    for k in (1, 3, 2):
        wait_spread(HIGH, k)
        first_amplitudes(pl.multiple_of(peers[k] * CHUNK, CHUNK))
    for k in (2, 1, 3):
        spread(LOW, k).start()

    def both_halves(q, carry):
        integrals = r.high[q].astype(jnp.float32) + r.low[q].astype(jnp.float32)
        r.integ[q] = integrals
        r.factor[q] = 2.0 * integrals - integrals.T
        return carry

    for sweep in range(ITERS):
        if sweep == ITERS - 1:
            for k in (1, 3, 2):
                wait_spread(LOW, k)
            lax.fori_loop(0, PAIRS, both_halves, 0, unroll=CHUNK)
        wait_halo(sweep)

        def update(q, sweep=sweep):
            firsts = [
                jnp.dot(
                    r.weighted[q, :, n * TILE : (n + 1) * TILE],
                    windows[sweep][jnp.clip(r.near[n, q] - (me - 1) * PAIRS, 0, 3 * PAIRS - 1)],
                    preferred_element_type=jnp.float32,
                ).astype(jnp.bfloat16)
                for n in range(4)
            ]
            coupled = lax.dot_general(
                jnp.concatenate(firsts, axis=1), r.vecs[q], (((1,), (1,)), ((), ())),
                preferred_element_type=jnp.float32,
            )
            integrals = r.high[q].astype(jnp.float32) if sweep < ITERS - 1 else r.integ[q]
            current = (coupled - integrals) * r.inverse[q]
            if sweep < ITERS - 1:
                windows[sweep + 1][PAIRS + q] = current.astype(jnp.bfloat16)
            else:
                r.amp[q] = current
                r.pair_energy[q] = jnp.sum(r.factor[q] * current)

        group = CHUNK if sweep < ITERS - 1 else 2 * CHUNK

        def some(j, carry, sweep=sweep, group=group):
            for i in range(group):
                update(j * group + i)
            if sweep < ITERS - 1:
                for side in range(2):
                    halo(sweep + 1, pl.multiple_of(j * CHUNK, CHUNK), CHUNK, side).start()
            return carry

        lax.fori_loop(0, PAIRS // group, some, 0)

    for k in range(1, AUXES):
        share(k).wait_send()
        for kind in (HIGH, LOW):
            spread(kind, k).wait_send()


def run_kernel(extra, table, count, occ, source, coef, energy, near, coupling, inter):
    exchanging = extra > 0
    smem, vmem = pl.BlockSpec(memory_space=pltpu.SMEM), pl.BlockSpec(memory_space=pltpu.VMEM)
    hbm = pl.BlockSpec(memory_space=pl.ANY)
    scratch = dict(SCRATCH, **(exchange_scratch(extra) if exchanging else {}))
    return pl.pallas_call(
        functools.partial(kernel, extra),
        out_shape=(
            jax.ShapeDtypeStruct((PAIRS, TILE, TILE), jnp.float32),
            jax.ShapeDtypeStruct((PAIRS,), jnp.float32),
        ),
        in_specs=[smem, smem, smem, vmem] + [hbm] * exchanging + [vmem, smem, smem, hbm],
        out_specs=(vmem, smem),
        scratch_shapes=[
            pltpu.SemaphoreType.DMA(v) if isinstance(v[0], int) else pltpu.VMEM(*v) for v in scratch.values()
        ],
        compiler_params=pltpu.CompilerParams(
            collective_id=extra, has_side_effects=True, vmem_limit_bytes=VMEM_LIMIT
        ),
    )(*([table, count, occ, source] + [coef] * exchanging + [energy, near, coupling, inter]))


def padded_exchange(blocks, coef, source_dev, block_pos, me):
    source = source_dev.reshape(OWNERS, TOTAL)
    position = block_pos.reshape(OWNERS, TOTAL)
    wanted = source == me
    ranking = jnp.cumsum(wanted.astype(jnp.int32), axis=1) - 1
    slots = jnp.arange(CAP, dtype=jnp.int32)
    chosen = wanted[:, None, :] & (ranking[:, None, :] == slots[None, :, None])
    send_pos = jnp.sum(jnp.where(chosen, position[:, None, :], 0), axis=2)
    incoming = lax.all_to_all(
        blocks[send_pos], "pair", split_axis=0, concat_axis=0, tiled=True
    )
    own_source = lax.dynamic_index_in_dim(source, me, 0, keepdims=False)
    order = jnp.arange(TOTAL, dtype=jnp.int32)
    earlier = (own_source[None, :] == own_source[:, None]) & (order[None, :] < order[:, None])
    own_rank = jnp.sum(earlier.astype(jnp.int32), axis=1)
    arrived = incoming.reshape((OWNERS * CAP,) + blocks.shape[1:])[own_source * CAP + own_rank]
    arrived = arrived.reshape((PAIRS, 2, DOM) + blocks.shape[1:])
    coefs = coef.reshape(PAIRS, DOM, TILE, TILE)
    projected = jnp.einsum(
        "qmtxp,qtpn->qmxn", arrived, coefs, preferred_element_type=jnp.float32
    ).astype(jnp.bfloat16)
    return jnp.einsum(
        "qxa,qxb->qab", projected[:, 0], projected[:, 1], preferred_element_type=jnp.float32
    )


def route_kernel(source, position, table, most, by_tile, taken):
    me = lax.axis_index("pair")
    plane, col = me // COLS, me % COLS
    lanes = PAIRS * COLS
    for c in range(REQ):
        for j in range(PLANES):
            cut = slice(j * lanes, (j + 1) * lanes)
            by_tile[0, c, j : j + 1, :] = source[c : c + 1, cut]
            by_tile[1, c, j : j + 1, :] = position[c : c + 1, cut]
    row = lax.broadcasted_iota(jnp.int32, (lanes, lanes), 0)
    lane = lax.broadcasted_iota(jnp.int32, (lanes, lanes), 1)
    earlier = ((row // PAIRS == lane // PAIRS) & (row < lane)).astype(jnp.float32)
    device = (row // PAIRS == lane).astype(jnp.float32)

    wanted = jnp.zeros((PLANES, lanes), jnp.float32)
    where = jnp.zeros((PLANES, lanes), jnp.float32)
    for c in range(REQ):
        hit = by_tile[0, c] == me
        wanted = wanted + jnp.where(hit, 1.0, 0.0)
        where = where + jnp.where(hit, by_tile[1, c].astype(jnp.float32), 0.0)
    rank = jnp.dot(wanted, earlier, preferred_element_type=jnp.float32)
    for s in range(CAP):
        chosen = jnp.where(rank == s, where, 0.0)
        table[SEND + s * PLANES : SEND + (s + 1) * PLANES, :] = jnp.dot(
            chosen, device, preferred_element_type=jnp.float32
        ).astype(jnp.int32)

    for s in range(OWNERS):
        count = jnp.zeros((PLANES, lanes), jnp.float32)
        for c in range(REQ):
            count = count + jnp.where(by_tile[0, c] == s, 1.0, 0.0)
        taken[s] = count
    counts = jnp.dot(
        taken[...].reshape(OWNERS * PLANES, lanes), device, preferred_element_type=jnp.float32
    )
    taken[...] = jnp.where(counts > DIRECT, 1.0, 0.0).reshape(OWNERS, PLANES, lanes)
    worst = jnp.zeros((PLANES, lanes), jnp.float32)
    for a in range(PLANES):
        total = taken[a * COLS]
        for k in range(1, COLS):
            total = total + taken[a * COLS + k]
        worst = jnp.maximum(worst, total)
    worst = jnp.max(worst).astype(jnp.int32)
    most[0] = worst

    planes = lax.broadcasted_iota(jnp.int32, (PLANES, lanes), 0)
    before = jnp.zeros((PLANES, lanes), jnp.float32)
    picked = [jnp.zeros((PLANES, lanes), jnp.int32) for _ in range(max(EXTRAS))]
    for k in range(COLS):
        third = taken[plane * COLS + k]
        back = lax.rem(k - col + COLS, COLS)
        for e in range(max(EXTRAS)):
            picked[e] = picked[e] + jnp.where((third > 0.0) & (before == e), back, 0)
        before = before + third
    for e in range(max(EXTRAS)):
        first = RELAY + e * PLANES
        table[first : first + PLANES, :] = picked[e] * PLANES + planes

    mine = source[:, pl.ds(pl.multiple_of(plane * lanes, lanes), lanes)]
    place = lax.broadcasted_iota(jnp.int32, (REQ, lanes), 1) % PAIRS

    def others(values, shift):
        if shift:
            inside = (place >= shift) & (place < PAIRS + shift)
            values = jnp.where(inside, pltpu.roll(values, shift % lanes, 1), -1)
        return [values] + [pltpu.roll(values, k, 0) for k in range(1, REQ)]

    own_rank = jnp.zeros((REQ, lanes), jnp.int32)
    for shift in range(1, PAIRS):
        for other in others(mine, shift):
            own_rank = own_rank + jnp.where(other == mine, 1, 0)
    thirds = jnp.where(own_rank >= DIRECT, mine, -1)
    first_of_plane = mine - mine % COLS
    extra_rank = jnp.zeros((REQ, lanes), jnp.int32)
    for shift in range(1 - PAIRS, PAIRS):
        for other in others(thirds, shift):
            extra_rank = extra_rank + jnp.where((other >= first_of_plane) & (other < mine), 1, 0)
    room = jnp.clip(worst, EXTRAS[0], EXTRAS[1])
    extra_row = (
        DIRECT * OWNERS
        + ((mine // COLS - plane + PLANES) % PLANES) * room
        + jnp.minimum(extra_rank, room - 1)
    )
    direct_row = ((mine - me + OWNERS) % OWNERS) * DIRECT + own_rank
    table[LAND : LAND + REQ, :] = jnp.where(own_rank >= DIRECT, extra_row, direct_row)


def route(source_dev, block_pos):
    vmem = pl.BlockSpec(memory_space=pltpu.VMEM)
    lanes = PAIRS * COLS
    return pl.pallas_call(
        route_kernel,
        out_shape=(
            jax.ShapeDtypeStruct((ROWS, lanes), jnp.int32),
            jax.ShapeDtypeStruct((1,), jnp.int32),
        ),
        in_specs=[vmem, vmem],
        out_specs=(vmem, pl.BlockSpec(memory_space=pltpu.SMEM)),
        scratch_shapes=[
            pltpu.VMEM((2, REQ, PLANES, lanes), jnp.int32),
            pltpu.VMEM((OWNERS, PLANES, lanes), jnp.float32),
        ],
    )(source_dev.T, block_pos.T)


def shards(
    blocks, pno_coef, source_dev, block_pos, pno_energy, occ_energy, pno_count, neighbour, coupling, intersection,
):
    me = lax.axis_index("pair")
    table, most = route(source_dev, block_pos)

    def finish(extra, source):
        return run_kernel(
            extra, table, pno_count, occ_energy, source, pno_coef, pno_energy, neighbour.T, coupling.T, intersection
        )

    return lax.switch(
        jnp.clip(most[0], 1, 3) - 1,
        [
            lambda: finish(1, blocks),
            lambda: finish(2, blocks),
            lambda: finish(0, padded_exchange(blocks, pno_coef, source_dev, block_pos, me)),
        ],
    )


def solution(mesh):
    return jax.shard_map(
        shards,
        mesh=mesh,
        in_specs=(
            P("pair", "aux", None),
            P("pair", None, None),
            P(),
            P(),
            P("pair", None),
            P("pair"),
            P("pair"),
            P("pair", None),
            P("pair", None),
            P("pair", None, None, None),
        ),
        out_specs=(P("pair", None, None), P("pair")),
        check_vma=False,
    )
```
